512 devices in a mesh: row: 16 (over z_lo, x), col: 32 (over z_hi, y, core).
Axes of the slice: x: 4, y: 8, z: 8 (z_hi: 2, z_lo: 4; z = z_hi * 4 + z_lo), core: 2. Of those that a mesh axis runs over, the one named last changes fastest.
Arguments:
- object_field: float32 [2, 4096, 8192], P(None, 'row', 'col'), may hold values from -6 to 6
- probe_modes: bfloat16 [2, 6, 256, 256], replicated, may hold values from -1.796875 to 1.796875
- offsets: int32 [16, 32, 1, 2], P('row', 'col'), may hold values from 0 to 255
- counts: int32 [16, 32], P('row', 'col'), may hold values from 0 to 1, as said below
- intensity: bfloat16 [16, 32, 1, 256, 256], P('row', 'col'), may hold values from 0 to 4
Outputs:
- object_new: float32 [2, 4096, 8192], P(None, 'row', 'col')
- probe_new: float32 [2, 6, 256, 256], P(None, None, 'row', 'col')
The draws below stay inside these ranges and needn't reach their ends.
Inputs may be any that keep to these rules, and one draw needn't show every extreme that they name: The first counts[a, b] slots of tile (a, b) are live and the others are ignored; some tile has 1 and some tile has none.
All inputs are finite; a program needn't handle non-finite values.
Results may differ from the reference program's by a relative error of at most 0.00045.
Values sent between devices are 32-bit elements; how exact they have to be, the bound alone decides.
No kernel may reach another device: no remote copies, remote signals or barrier semaphores. Data moves between devices by JAX's collectives and lax.ppermute only.
A program may use at most 64 MiB of HBM per device.

```python
import jax
import jax.numpy as jnp
from jax import lax

MODES = 6
PATCH = 256
TILE = 256
SLOTS = 1
NY = 4096
NX = 8192
N_ROW = 16
N_COL = 32


def draw_counts(key, part):
    key = jax.random.fold_in(key, 7)
    key_base, key_row, key_col = jax.random.split(key, 3)
    levels = jax.random.randint(key_base, (N_ROW, N_COL), 0, SLOTS + 1, dtype=jnp.int32)
    row_pick = jax.random.randint(key_row, (), 0, N_ROW, dtype=jnp.int32)
    col_pick = jax.random.randint(key_col, (), 0, N_COL, dtype=jnp.int32)
    levels = levels.at[row_pick, col_pick].set(SLOTS)
    levels = levels.at[row_pick, (col_pick + 1) % N_COL].set(0)
    return levels


def set_ends(drawn, rng, least, high):
    dims = drawn.shape
    place = [jax.random.randint(jax.random.fold_in(rng, axis), (), 0, dims[axis]) for axis in range(len(dims))]
    drawn = drawn.at[tuple(place)].set(least)
    longest = dims.index(max(dims))
    place[longest] = (place[longest] + 1) % dims[longest]
    return drawn.at[tuple(place)].set(high)


def shard_levels(rng, extent, pieces, low, high):
    loudness, own = 1.0, jax.random.fold_in(rng, 6)
    for position, parts in pieces:
        draws = jnp.exp(jax.random.uniform(jax.random.fold_in(own, position), (parts,), jnp.float32, low / len(pieces), high / len(pieces)))
        loudness = loudness * jnp.repeat(draws, extent[position] // parts).reshape([-1 if axis == position else 1 for axis in range(len(extent))])
    return loudness


def centred(key, extent, deviation, reach, cuts=(), held_as=jnp.bfloat16):
    values = deviation * jax.random.normal(key, extent, jnp.float32)
    if cuts:
        values = values * shard_levels(key, extent, cuts, -0.22, 0.18)
    return jnp.clip(values, -reach, reach).astype(held_as)


def setup_inputs(seed: int = 0) -> dict:
    arg_keys = jax.random.split(jax.random.key(seed), 6)
    return {
        "object_field": centred(arg_keys[0], (2, NY, NX), 1.0, 6.0, ((1, 16), (2, 32)), jnp.float32),
        "probe_modes": centred(arg_keys[1], (2, MODES, PATCH, PATCH), 0.3, 1.796875),
        "offsets": set_ends(jax.random.randint(arg_keys[2], (N_ROW, N_COL, SLOTS, 2), 0, TILE), jax.random.fold_in(arg_keys[2], 1), 0, TILE - 1).astype(jnp.int32),
        "counts": draw_counts(jax.random.fold_in(arg_keys[5], 71), 0),
        "intensity": jnp.clip(4.0 * jax.random.uniform(arg_keys[4], (N_ROW, N_COL, SLOTS, PATCH, PATCH), jnp.float32) ** shard_levels(arg_keys[4], (N_ROW, N_COL, SLOTS, PATCH, PATCH), ((0, 16), (1, 32)), -0.2, 0.2), 0.0, 4.0).astype(jnp.bfloat16),
    }


object_rate = 0.25


def reference(object_field, probe_modes, offsets, counts, intensity):
    probe_full = probe_modes.astype(jnp.float32)
    probe_cplx = lax.complex(probe_full[0], probe_full[1])
    padded = jnp.pad(object_field, ((0, 0), (0, PATCH), (0, PATCH)))
    row_anchor = jnp.arange(N_ROW, dtype=jnp.int32)[:, None, None] * TILE
    col_anchor = jnp.arange(N_COL, dtype=jnp.int32)[None, :, None] * TILE
    anchors_y = (row_anchor + offsets[..., 0]).reshape(-1).astype(jnp.int32)
    anchors_x = (col_anchor + offsets[..., 1]).reshape(-1).astype(jnp.int32)
    live_flags = (jnp.arange(SLOTS, dtype=jnp.int32)[None, None, :] < counts[:, :, None]).astype(jnp.float32).reshape(-1)
    measured = intensity.reshape(-1, PATCH, PATCH)

    def advance(state_pair, slot_item):
        grad_field, probe_grad = state_pair
        anchor_y, anchor_x, live_flag, measured_slot = slot_item
        start = (jnp.int32(0), anchor_y, anchor_x)
        window = lax.dynamic_slice(padded, start, (2, PATCH, PATCH))
        obj_patch = lax.complex(window[0], window[1])
        far_field = jnp.fft.fft2(probe_cplx * obj_patch[None], norm="ortho")
        summed = jnp.sum(far_field.real * far_field.real + far_field.imag * far_field.imag, axis=0)
        residual = summed - measured_slot.astype(jnp.float32)
        near_field = jnp.fft.ifft2(residual[None] * far_field, norm="ortho") * live_flag
        obj_step = jnp.sum(jnp.conj(probe_cplx) * near_field, axis=0)
        probe_step = jnp.conj(obj_patch)[None] * near_field
        current = lax.dynamic_slice(grad_field, start, (2, PATCH, PATCH))
        update_pair = jnp.stack([obj_step.real, obj_step.imag])
        grad_field = lax.dynamic_update_slice(grad_field, current + update_pair, start)
        probe_grad = probe_grad + jnp.stack([probe_step.real, probe_step.imag])
        return (grad_field, probe_grad), None

    initial = (jnp.zeros(padded.shape, jnp.float32), jnp.zeros(probe_full.shape, jnp.float32))
    (grad_field, probe_grad), unused = lax.scan(advance, initial, (anchors_y, anchors_x, live_flags, measured))
    object_new = object_field - object_rate * grad_field[:, :NY, :NX]
    probe_rate = (N_ROW * N_COL * SLOTS) ** -0.5
    probe_new = probe_full - probe_rate * probe_grad
    return (object_new, probe_new)
```

```python
import functools
import math

import jax
import jax.numpy as jnp
import ml_dtypes
import numpy as np
from jax import lax
from jax.experimental import pallas as pl
from jax.experimental.pallas import tpu as pltpu
from jax.sharding import PartitionSpec as P

object_rate = 0.25
f32 = jnp.float32
bf16 = jnp.bfloat16
half = 128
full = 256
modes = 6
strip = 16


def passed_along(x, axis, by):
    devices = lax.axis_size(axis)
    pairs = [(i, i + by) for i in range(devices) if 0 <= i + by < devices]
    return lax.ppermute(x, axis, pairs)


def halves_tables():
    place = np.arange(half)[:, None]
    freq = np.arange(half)[None, :]
    columns = column_order()[:half]
    tables = []
    for places in (place, columns[:, None]):
        for odd in (0, 1):
            angle = -2.0 * math.pi * ((places * (2 * freq + odd)) % full) / full
            re, im = np.cos(angle) / 16.0, np.sin(angle) / 16.0
            real_form = np.block([[re, im], [-im, re]]).astype(np.float32)
            for form in (real_form, real_form.T):
                high = form.astype(ml_dtypes.bfloat16)
                low = (form - high.astype(np.float32)).astype(ml_dtypes.bfloat16)
                tables.append(np.stack([high, low]))
    frequencies = np.zeros((full, full), np.float32)
    shuffle = np.zeros((full, full), np.float32)
    for k in range(full):
        frequencies[(k % 2) * half + k // 2, k] = 1.0
    shuffle[column_order(), np.arange(full)] = 1.0
    orders = np.stack([frequencies, frequencies.T, shuffle, shuffle.T])
    return np.stack(tables), orders.astype(ml_dtypes.bfloat16)


def column_order():
    columns = np.arange(full).reshape(2, 8, 2, 8)
    return columns.transpose(0, 2, 1, 3).reshape(-1)


def split(x):
    high = x.astype(bf16)
    return high, (x - high.astype(f32)).astype(bf16)


def dot(a, b):
    return jnp.dot(a, b, preferred_element_type=f32)


def data_by_table(x, table_ref, which):
    high, low = split(x)
    table_high, table_low = table_ref[which, 0], table_ref[which, 1]
    return dot(
        jnp.concatenate([high, high, low], axis=1),
        jnp.concatenate([table_high, table_low, table_high], axis=0),
    )


def table_by_data(table_ref, which, x):
    high, low = split(x)
    table_high, table_low = table_ref[which, 0], table_ref[which, 1]
    return dot(
        jnp.concatenate([table_high, table_low, table_high], axis=1),
        jnp.concatenate([high, high, low], axis=0),
    )


def forward(exit_re, exit_im, table_ref):
    rows = []
    for sign, which in ((1.0, 0), (-1.0, 2)):
        folded = jnp.concatenate(
            [
                exit_re[:, :half] + sign * exit_re[:, half:],
                exit_im[:, :half] + sign * exit_im[:, half:],
            ],
            axis=1,
        )
        rows.append(data_by_table(folded, table_ref, 4 + which))
    even, odd = rows
    outs = []
    for sign, which in ((1.0, 1), (-1.0, 3)):
        fold_even = even[:half] + sign * even[half:]
        fold_odd = odd[:half] + sign * odd[half:]
        stacked = jnp.concatenate(
            [
                jnp.concatenate([fold_even[:, :half], fold_odd[:, :half]], axis=1),
                jnp.concatenate([fold_even[:, half:], fold_odd[:, half:]], axis=1),
            ],
            axis=0,
        )
        outs.append(table_by_data(table_ref, which, stacked))
    return outs


def backward(even, odd, table_ref):
    part_even = table_by_data(table_ref, 0, even)
    part_odd = table_by_data(table_ref, 2, odd)
    upper = part_even + part_odd
    lower = part_even - part_odd
    rows_re = jnp.concatenate([upper[:half], lower[:half]], axis=0)
    rows_im = jnp.concatenate([upper[half:], lower[half:]], axis=0)
    cols_even = data_by_table(
        jnp.concatenate([rows_re[:, :half], rows_im[:, :half]], axis=1), table_ref, 5
    )
    cols_odd = data_by_table(
        jnp.concatenate([rows_re[:, half:], rows_im[:, half:]], axis=1), table_ref, 7
    )
    near_re = jnp.concatenate(
        [cols_even[:, :half] + cols_odd[:, :half], cols_even[:, :half] - cols_odd[:, :half]], axis=1
    )
    near_im = jnp.concatenate(
        [cols_even[:, half:] + cols_odd[:, half:], cols_even[:, half:] - cols_odd[:, half:]], axis=1
    )
    return near_re, near_im


def reorder(x, order):
    high = x.astype(bf16)
    left = x - high.astype(f32)
    mid = left.astype(bf16)
    low = (left - mid.astype(f32)).astype(bf16)
    return dot(jnp.concatenate([high, mid, low], axis=1), jnp.concatenate([order, order, order], axis=0))


def store_strips(mine_ref, peer_ref, index, value, core):
    left, right = value[:, :half], value[:, half:]
    lanes = lax.broadcasted_iota(jnp.int32, (full, half), 1)
    first = jnp.where(lanes < half // 2, left, pltpu.roll(right, half // 2, 1))
    second = jnp.where(lanes < half // 2, pltpu.roll(left, half // 2, 1), right)
    mine = jnp.where(core == 0, first, second)
    peer = jnp.where(core == 0, second, first)
    for z in range(4):
        for x in range(4):
            at = (z * 4 + x) * strip
            mine_ref[x, z, index] = mine[at : at + strip]
            peer_ref[x, z, index] = peer[at : at + strip]


def cells():
    rows = lax.broadcasted_iota(jnp.int32, (full, full), 0)
    cols = lax.broadcasted_iota(jnp.int32, (full, full), 1)
    return rows, cols


def prepare_kernel(probe_ref, intensity_ref, table_ref, order_ref, probe_out, measured_out, table_out, order_out):
    frequencies, turned, shuffle = order_ref[0], order_ref[1], order_ref[2]
    measured_out[...] = dot(dot(frequencies, intensity_ref[...]).astype(bf16), turned)
    for part in range(2):
        for mode in range(modes):
            probe_out[part, mode] = dot(probe_ref[part, mode], shuffle).astype(bf16)
    table_out[...] = table_ref[...]
    order_out[0] = shuffle
    order_out[1] = order_ref[3]


def main_kernel(
    offset_ref, count_ref, own_ref, right_ref, below_ref, diag_ref, probe_ref, measured_ref, table_ref, order_ref,
    mine_ref, peer_ref, upper_ref, lower_ref, window_ref, far_ref,
):
    row_offset = offset_ref[0]
    col_offset = offset_ref[1]
    live = (count_ref[0] > 0).astype(f32)
    core = lax.axis_index("core")
    rows, cols = cells()
    in_row = rows >= row_offset
    in_col = cols >= col_offset
    for part in range(2):
        upper = jnp.where(in_col, own_ref[part], right_ref[part])
        lower = jnp.where(in_col, below_ref[part], diag_ref[part])
        mixed = jnp.where(in_row, upper, lower)
        mixed = pltpu.roll(mixed, lax.rem(full - row_offset, full), 0)
        window_ref[part] = reorder(pltpu.roll(mixed, lax.rem(full - col_offset, full), 1), order_ref[0])
    sum_even = -measured_ref[:half]
    sum_odd = -measured_ref[half:]
    for mode in range(modes):
        win_re, win_im = window_ref[0], window_ref[1]
        probe_re = probe_ref[0, mode].astype(f32)
        probe_im = probe_ref[1, mode].astype(f32)
        even, odd = forward(
            probe_re * win_re - probe_im * win_im, probe_re * win_im + probe_im * win_re, table_ref
        )
        far_ref[mode, 0] = even
        far_ref[mode, 1] = odd
        sum_even = sum_even + (even[:half] * even[:half] + even[half:] * even[half:])
        sum_odd = sum_odd + (odd[:half] * odd[:half] + odd[half:] * odd[half:])
    sum_even = sum_even * live
    sum_odd = sum_odd * live
    res_even = jnp.concatenate([sum_even, sum_even], axis=0)
    res_odd = jnp.concatenate([sum_odd, sum_odd], axis=0)
    obj_re = jnp.zeros((full, full), f32)
    obj_im = jnp.zeros((full, full), f32)
    for mode in range(modes):
        win_re, win_im = window_ref[0], window_ref[1]
        probe_re = probe_ref[0, mode].astype(f32)
        probe_im = probe_ref[1, mode].astype(f32)
        near_re, near_im = backward(far_ref[mode, 0] * res_even, far_ref[mode, 1] * res_odd, table_ref)
        store_strips(mine_ref, peer_ref, mode, win_re * near_re + win_im * near_im, core)
        store_strips(mine_ref, peer_ref, modes + mode, win_re * near_im - win_im * near_re, core)
        obj_re = obj_re + probe_re * near_re + probe_im * near_im
        obj_im = obj_im + probe_re * near_im - probe_im * near_re
    for part, total in enumerate((obj_re, obj_im)):
        placed = reorder(total, order_ref[1])
        placed = pltpu.roll(pltpu.roll(placed, row_offset, 0), col_offset, 1)
        upper_ref[part] = jnp.where(in_row, placed, 0.0)
        lower_ref[part] = jnp.where(in_row, 0.0, placed)


def cores_kernel(mine_ref, theirs_ref, send_ref, keep_ref):
    x = lax.axis_index("x")
    core = lax.axis_index("core")
    first = jnp.where(core == 0, x ^ 1, 3 - x)
    second = jnp.where(core == 0, 3 - x, x ^ 1)
    for ref, slot, index in ((send_ref, 0, first), (send_ref, 1, x ^ 2), (keep_ref, 0, x), (keep_ref, 1, second)):
        ref[slot] = mine_ref[index] + theirs_ref[index]


def columns_kernel(kept_ref, got_ref, came_ref, out_ref):
    lanes = lax.broadcasted_iota(jnp.int32, (96, half), 1)
    for z in range(4):
        total = (kept_ref[0, z] + got_ref[0, z] + came_ref[z]).reshape(192, half)
        top, bottom = total[:96], total[96:]
        out_ref[2 * z] = jnp.where(lanes < half // 2, top, pltpu.roll(bottom, half // 2, 1))
        out_ref[2 * z + 1] = jnp.where(lanes < half // 2, pltpu.roll(top, half // 2, 1), bottom)


def turn_kernel(parts_ref, out_ref):
    total = parts_ref[0]
    for i in range(1, 8):
        total = total + parts_ref[i]
    turned = total.T
    for part in range(2):
        for y in range(8):
            at = part * 64 + y * 8
            out_ref[y, part * 8 : part * 8 + 8] = turned[at : at + 8]


def shaped(*shape, dtype=f32):
    return jax.ShapeDtypeStruct(shape, dtype)


vmem = pl.BlockSpec(memory_space=pltpu.VMEM)
smem = pl.BlockSpec(memory_space=pltpu.SMEM)


def call(kernel, name, inputs, outputs, scratch=(), flops=0, moved=0, limit=16):
    return pl.pallas_call(
        kernel,
        out_shape=tuple(outputs) if len(outputs) > 1 else outputs[0],
        in_specs=inputs,
        out_specs=(vmem,) * len(outputs) if len(outputs) > 1 else vmem,
        scratch_shapes=scratch,
        compiler_params=pltpu.CompilerParams(vmem_limit_bytes=limit * 1024 * 1024),
        cost_estimate=pl.CostEstimate(flops=flops, bytes_accessed=moved, transcendentals=0),
        name=name,
    )


def local(object_field, probe_modes, offsets, counts, intensity):
    rows = ("z_lo", "x")
    cols = ("z_hi", "y", "core")
    tables, orders = halves_tables()
    below = passed_along(object_field, rows, -1)
    right = passed_along(object_field, cols, -1)
    diag = passed_along(below, cols, -1)
    above_offset = passed_along(offsets[:, :, :, 1], rows, 1)
    probe, measured, table, order = call(
        prepare_kernel,
        "prepare",
        [vmem] * 4,
        [
            shaped(2, modes, full, full, dtype=bf16),
            shaped(full, full),
            shaped(8, 2, full, full, dtype=bf16),
            shaped(2, full, full, dtype=bf16),
        ],
        flops=500_000_000,
        moved=8_000_000,
    )(probe_modes, intensity[0, 0, 0], jnp.asarray(tables), jnp.asarray(orders))
    block_shape = (4, 4, 2 * modes, strip, half)
    mine, peer, upper, lower = call(
        main_kernel,
        "step",
        [smem, smem] + [vmem] * 8,
        [shaped(*block_shape), shaped(*block_shape), shaped(2, full, full), shaped(2, full, full)],
        scratch=[pltpu.VMEM((2, full, full), f32), pltpu.VMEM((modes, 2, full, full), f32)],
        flops=5_000_000_000,
        moved=12_000_000,
        limit=24,
    )(offsets.reshape(2), counts.reshape(1), object_field, right, below, diag, probe, measured, table, order)

    theirs = lax.ppermute(peer, "core", [(0, 1), (1, 0)])
    from_above = passed_along(lower, rows, 1)
    half_shape = (2, *block_shape[1:])
    send, keep = call(
        cores_kernel, "add_cores", [vmem] * 2, [shaped(*half_shape)] * 2, moved=6_000_000
    )(mine, theirs)
    near_pairs = [(2 * x + c, 2 * ((x ^ 1) if c == 0 else 3 - x) + c) for x in range(4) for c in range(2)]
    far_pairs = [(2 * x + c, 2 * (3 - x if c == 0 else (x ^ 1)) + c) for x in range(4) for c in range(2)]
    got = lax.ppermute(send, ("x", "core"), near_pairs)
    came = lax.ppermute(keep[1] + got[1], ("x", "core"), far_pairs)
    packed = call(columns_kernel, "add_columns", [vmem] * 3, [shaped(8, 96, half)], moved=2_000_000)(keep, got, came)
    parts = lax.all_to_all(packed, ("z_lo", "z_hi"), 0, 0, tiled=True)
    turned = call(turn_kernel, "add_turn", [vmem], [shaped(8, strip, 96)], moved=500_000)(parts)
    parts = lax.all_to_all(turned, "y", 0, 0, tiled=True)
    share = jnp.sum(parts, axis=0).reshape(2, 8, modes, strip).transpose(0, 2, 3, 1)
    start = (0, 0, lax.axis_index(rows) * strip, lax.axis_index(cols) * 8)
    own_probe = lax.dynamic_slice(probe_modes, start, (2, modes, strip, 8)).astype(f32)
    probe_new = own_probe - (512.0 ** -0.5) * share

    lanes = lax.broadcasted_iota(jnp.int32, (2, full, full), 2)
    stays = lanes >= offsets[0, 0, 0, 1]
    above_stays = lanes >= above_offset[0, 0, 0]
    zero = jnp.zeros((), f32)
    moves = jnp.where(stays, zero, upper) + jnp.where(above_stays, zero, from_above)
    from_left = passed_along(moves, cols, 1)
    held = jnp.where(stays, upper, zero) + jnp.where(above_stays, from_above, zero)
    object_new = object_field - object_rate * (held + from_left)
    return (object_new, probe_new)


def solution(mesh):
    grid = jax.sharding.Mesh(mesh.devices.reshape(4, 4, 2, 8, 2), ("z_lo", "x", "z_hi", "y", "core"))
    rows = ("z_lo", "x")
    cols = ("z_hi", "y", "core")
    in_specs = (
        P(None, rows, cols),
        P(),
        P(rows, cols, None, None),
        P(rows, cols),
        P(rows, cols, None, None, None),
    )
    out_specs = (P(None, rows, cols), P(None, None, rows, cols))
    return jax.shard_map(local, mesh=grid, in_specs=in_specs, out_specs=out_specs, check_vma=False)
```

```python
import functools
import math

import jax
import jax.numpy as jnp
import ml_dtypes
import numpy as np
from jax import lax
from jax.experimental import pallas as pl
from jax.experimental.pallas import tpu as pltpu
from jax.sharding import PartitionSpec as P

object_rate = 0.25
f32 = jnp.float32
bf16 = jnp.bfloat16
half = 128
full = 256
modes = 6
strip = 16


def passed_along(x, axis, by):
    devices = lax.axis_size(axis)
    pairs = [(i, i + by) for i in range(devices) if 0 <= i + by < devices]
    return lax.ppermute(x, axis, pairs)


def halves_tables():
    place = np.arange(half)[:, None]
    freq = np.arange(half)[None, :]
    columns = column_order()[:half]
    tables = []
    for places in (place, columns[:, None]):
        for odd in (0, 1):
            angle = -2.0 * math.pi * ((places * (2 * freq + odd)) % full) / full
            re, im = np.cos(angle) / 16.0, np.sin(angle) / 16.0
            real_form = np.block([[re, im], [-im, re]]).astype(np.float32)
            for form in (real_form, real_form.T):
                high = form.astype(ml_dtypes.bfloat16)
                low = (form - high.astype(np.float32)).astype(ml_dtypes.bfloat16)
                tables.append(np.stack([high, low]))
    frequencies = np.zeros((full, full), np.float32)
    shuffle = np.zeros((full, full), np.float32)
    for k in range(full):
        frequencies[(k % 2) * half + k // 2, k] = 1.0
    shuffle[column_order(), np.arange(full)] = 1.0
    orders = np.stack([frequencies, frequencies.T, shuffle, shuffle.T])
    return np.stack(tables), orders.astype(ml_dtypes.bfloat16)


def column_order():
    columns = np.arange(full).reshape(2, 8, 2, 8)
    return columns.transpose(0, 2, 1, 3).reshape(-1)


def split(x):
    high = x.astype(bf16)
    return high, (x - high.astype(f32)).astype(bf16)


def dot(a, b):
    return jnp.dot(a, b, preferred_element_type=f32)


def data_by_table(x, table_ref, which):
    high, low = split(x)
    table_high, table_low = table_ref[which, 0], table_ref[which, 1]
    return dot(
        jnp.concatenate([high, high, low], axis=1),
        jnp.concatenate([table_high, table_low, table_high], axis=0),
    )


def table_by_data(table_ref, which, x):
    high, low = split(x)
    table_high, table_low = table_ref[which, 0], table_ref[which, 1]
    return dot(
        jnp.concatenate([table_high, table_low, table_high], axis=1),
        jnp.concatenate([high, high, low], axis=0),
    )


def forward(exit_re, exit_im, table_ref):
    rows = []
    for sign, which in ((1.0, 0), (-1.0, 2)):
        folded = jnp.concatenate(
            [
                exit_re[:, :half] + sign * exit_re[:, half:],
                exit_im[:, :half] + sign * exit_im[:, half:],
            ],
            axis=1,
        )
        rows.append(data_by_table(folded, table_ref, 4 + which))
    even, odd = rows
    outs = []
    for sign, which in ((1.0, 1), (-1.0, 3)):
        fold_even = even[:half] + sign * even[half:]
        fold_odd = odd[:half] + sign * odd[half:]
        stacked = jnp.concatenate(
            [
                jnp.concatenate([fold_even[:, :half], fold_odd[:, :half]], axis=1),
                jnp.concatenate([fold_even[:, half:], fold_odd[:, half:]], axis=1),
            ],
            axis=0,
        )
        outs.append(table_by_data(table_ref, which, stacked))
    return outs


def backward(even, odd, table_ref):
    part_even = table_by_data(table_ref, 0, even)
    part_odd = table_by_data(table_ref, 2, odd)
    upper = part_even + part_odd
    lower = part_even - part_odd
    rows_re = jnp.concatenate([upper[:half], lower[:half]], axis=0)
    rows_im = jnp.concatenate([upper[half:], lower[half:]], axis=0)
    cols_even = data_by_table(
        jnp.concatenate([rows_re[:, :half], rows_im[:, :half]], axis=1), table_ref, 5
    )
    cols_odd = data_by_table(
        jnp.concatenate([rows_re[:, half:], rows_im[:, half:]], axis=1), table_ref, 7
    )
    near_re = jnp.concatenate(
        [cols_even[:, :half] + cols_odd[:, :half], cols_even[:, :half] - cols_odd[:, :half]], axis=1
    )
    near_im = jnp.concatenate(
        [cols_even[:, half:] + cols_odd[:, half:], cols_even[:, half:] - cols_odd[:, half:]], axis=1
    )
    return near_re, near_im


def reorder(x, order):
    high = x.astype(bf16)
    left = x - high.astype(f32)
    mid = left.astype(bf16)
    low = (left - mid.astype(f32)).astype(bf16)
    return dot(jnp.concatenate([high, mid, low], axis=1), jnp.concatenate([order, order, order], axis=0))


def store_strips(mine_ref, peer_ref, index, value, core):
    left, right = value[:, :half], value[:, half:]
    lanes = lax.broadcasted_iota(jnp.int32, (full, half), 1)
    first = jnp.where(lanes < half // 2, left, pltpu.roll(right, half // 2, 1))
    second = jnp.where(lanes < half // 2, pltpu.roll(left, half // 2, 1), right)
    mine = jnp.where(core == 0, first, second)
    peer = jnp.where(core == 0, second, first)
    for z in range(4):
        for x in range(4):
            at = (z * 4 + x) * strip
            mine_ref[x, z, index] = mine[at : at + strip]
            peer_ref[x, z, index] = peer[at : at + strip]


def cells():
    rows = lax.broadcasted_iota(jnp.int32, (full, full), 0)
    cols = lax.broadcasted_iota(jnp.int32, (full, full), 1)
    return rows, cols


def prepare_kernel(
    probe_in, intensity_in, table_in, order_in, probe_out, measured_out, table_out, order_out,
    probe_ref, intensity_ref, order_ref, sems,
):
    copies = [
        pltpu.make_async_copy(source, target, sems.at[i])
        for i, (source, target) in enumerate(
            [(order_in, order_ref), (intensity_in, intensity_ref), (probe_in, probe_ref), (table_in, table_out)]
        )
    ]
    for copy in copies:
        copy.start()
    copies[0].wait()
    copies[1].wait()
    frequencies, turned, shuffle = order_ref[0], order_ref[1], order_ref[2]
    measured_out[...] = dot(dot(frequencies, intensity_ref[...]).astype(bf16), turned)
    order_out[0] = shuffle
    order_out[1] = order_ref[3]
    copies[2].wait()
    for part in range(2):
        for mode in range(modes):
            probe_out[part, mode] = dot(probe_ref[part, mode], shuffle).astype(bf16)
    copies[3].wait()


def main_kernel(
    offset_ref, count_ref, own_re, own_im, right_re, right_im, lower_re, lower_im, probe_ref, measured_ref,
    table_ref, order_ref, mine_re_ref, mine_im_ref, peer_re_ref, peer_im_ref, stays_ref, moves_ref,
    window_ref, far_ref,
):
    row_offset = offset_ref[0]
    col_offset = offset_ref[1]
    live = (count_ref[0] > 0).astype(f32)
    core = lax.axis_index("core")
    rows, cols = cells()
    in_row = rows >= row_offset
    in_col = cols >= col_offset
    parts = ((own_re, right_re, lower_re), (own_im, right_im, lower_im))
    for part, (own_ref, right_ref, lower_ref) in enumerate(parts):
        mixed = jnp.where(in_row, jnp.where(in_col, own_ref[...], right_ref[...]), lower_ref[...])
        mixed = pltpu.roll(mixed, lax.rem(full - row_offset, full), 0)
        window_ref[part] = reorder(pltpu.roll(mixed, lax.rem(full - col_offset, full), 1), order_ref[0])
    sum_even = -measured_ref[:half]
    sum_odd = -measured_ref[half:]
    for mode in range(modes):
        win_re, win_im = window_ref[0], window_ref[1]
        probe_re = probe_ref[0, mode].astype(f32)
        probe_im = probe_ref[1, mode].astype(f32)
        even, odd = forward(
            probe_re * win_re - probe_im * win_im, probe_re * win_im + probe_im * win_re, table_ref
        )
        far_ref[mode, 0] = even
        far_ref[mode, 1] = odd
        sum_even = sum_even + (even[:half] * even[:half] + even[half:] * even[half:])
        sum_odd = sum_odd + (odd[:half] * odd[:half] + odd[half:] * odd[half:])
    sum_even = sum_even * live
    sum_odd = sum_odd * live
    res_even = jnp.concatenate([sum_even, sum_even], axis=0)
    res_odd = jnp.concatenate([sum_odd, sum_odd], axis=0)
    obj_re = jnp.zeros((full, full), f32)
    obj_im = jnp.zeros((full, full), f32)
    for mode in range(modes):
        win_re, win_im = window_ref[0], window_ref[1]
        probe_re = probe_ref[0, mode].astype(f32)
        probe_im = probe_ref[1, mode].astype(f32)
        near_re, near_im = backward(far_ref[mode, 0] * res_even, far_ref[mode, 1] * res_odd, table_ref)
        store_strips(mine_re_ref, peer_re_ref, mode, win_re * near_re + win_im * near_im, core)
        store_strips(mine_im_ref, peer_im_ref, mode, win_re * near_im - win_im * near_re, core)
        obj_re = obj_re + probe_re * near_re + probe_im * near_im
        obj_im = obj_im + probe_re * near_im - probe_im * near_re
    for part, total in enumerate((obj_re, obj_im)):
        placed = reorder(total, order_ref[1])
        placed = pltpu.roll(pltpu.roll(placed, row_offset, 0), col_offset, 1)
        stays_ref[part] = jnp.where(in_col, placed, 0.0)
        moves_ref[part, :full] = jnp.where(in_col, 0.0, placed)
        moves_ref[part, full:] = jnp.zeros((8, full), f32) + row_offset.astype(f32)


def mix_kernel(offset_ref, own_ref, right_ref, out_ref):
    rows, cols = cells()
    out_ref[...] = jnp.where(cols >= offset_ref[1], own_ref[...], right_ref[...])


def down_kernel(offset_ref, stays_ref, moved_ref, down_ref, held_ref):
    rows, cols = cells()
    in_row = rows >= offset_ref[0]
    left_in_row = rows.astype(f32) >= moved_ref[0, full : full + 1]
    for part in range(2):
        stays, moved = stays_ref[part], moved_ref[part, :full]
        down_ref[part] = jnp.where(in_row, 0.0, stays) + jnp.where(left_in_row, 0.0, moved)
        held_ref[part] = jnp.where(in_row, stays, 0.0) + jnp.where(left_in_row, moved, 0.0)


def cores_kernel(mine_ref, theirs_ref, send_ref, keep_ref):
    x = lax.axis_index("x")
    core = lax.axis_index("core")
    first = jnp.where(core == 0, x ^ 1, 3 - x)
    second = jnp.where(core == 0, 3 - x, x ^ 1)
    for ref, slot, index in ((send_ref, 0, first), (send_ref, 1, x ^ 2), (keep_ref, 0, x), (keep_ref, 1, second)):
        ref[slot] = mine_ref[index] + theirs_ref[index]


def columns_kernel(kept_re, got_re, came_re, kept_im, got_im, came_im, out_ref):
    for part, (kept_ref, got_ref, came_ref) in enumerate(((kept_re, got_re, came_re), (kept_im, got_im, came_im))):
        for z in range(4):
            turned = (kept_ref[0, z] + got_ref[0, z] + came_ref[z]).reshape(96, half).T
            lane = z * 192 + part * 96
            for y in range(8):
                for z_hi in range(2):
                    at = z_hi * 64 + y * 8
                    out_ref[y, z_hi * 8 : z_hi * 8 + 8, lane : lane + 96] = turned[at : at + 8]


def depth_kernel(parts_ref, out_ref):
    total = parts_ref[0]
    for i in range(1, 8):
        total = total + parts_ref[i]
    for z in range(4):
        for z_hi in range(2):
            out_ref[2 * z + z_hi] = total[z_hi * 8 : z_hi * 8 + 8, z * 192 : z * 192 + 192]


def shaped(*shape, dtype=f32):
    return jax.ShapeDtypeStruct(shape, dtype)


vmem = pl.BlockSpec(memory_space=pltpu.VMEM)
smem = pl.BlockSpec(memory_space=pltpu.SMEM)


def call(kernel, name, inputs, outputs, scratch=(), flops=0, moved=0, limit=16):
    return pl.pallas_call(
        kernel,
        out_shape=tuple(outputs) if len(outputs) > 1 else outputs[0],
        in_specs=inputs,
        out_specs=(vmem,) * len(outputs) if len(outputs) > 1 else vmem,
        scratch_shapes=scratch,
        compiler_params=pltpu.CompilerParams(vmem_limit_bytes=limit * 1024 * 1024),
        cost_estimate=pl.CostEstimate(flops=flops, bytes_accessed=moved, transcendentals=0),
        name=name,
    )


def local(object_field, probe_modes, offsets, counts, intensity):
    rows = ("z_lo", "x")
    cols = ("z_hi", "y", "core")
    tables, orders = halves_tables()
    above_offset = passed_along(offsets, rows, 1).reshape(2)
    own = (object_field[0], object_field[1])
    above_offset, *own = lax.optimization_barrier((above_offset, *own))
    right = [passed_along(part, cols, -1) for part in own]
    lower = []
    for part, beside in zip(own, right):
        mixed = call(mix_kernel, "mix", [smem, vmem, vmem], [shaped(full, full)], moved=1_000_000)(
            above_offset, part, beside
        )
        lower.append(passed_along(mixed, rows, -1))
    start = (0, 0, lax.axis_index(rows) * strip, lax.axis_index(cols) * 8)
    own_probe = lax.dynamic_slice(probe_modes, start, (2, modes, strip, 8)).astype(f32)
    probe, measured, table, order = call(
        prepare_kernel,
        "prepare",
        [pl.BlockSpec(memory_space=pl.ANY)] * 4,
        [
            shaped(2, modes, full, full, dtype=bf16),
            shaped(full, full),
            shaped(8, 2, full, full, dtype=bf16),
            shaped(2, full, full, dtype=bf16),
        ],
        scratch=[
            pltpu.VMEM((2, modes, full, full), bf16),
            pltpu.VMEM((full, full), bf16),
            pltpu.VMEM((4, full, full), bf16),
            pltpu.SemaphoreType.DMA((4,)),
        ],
        flops=500_000_000,
        moved=8_000_000,
    )(probe_modes, intensity[0, 0, 0], jnp.asarray(tables), jnp.asarray(orders))
    block_shape = (4, 4, modes, strip, half)
    mine_re, mine_im, peer_re, peer_im, stays, moves = call(
        main_kernel,
        "step",
        [smem, smem] + [vmem] * 10,
        [shaped(*block_shape)] * 4 + [shaped(2, full, full), shaped(2, full + 8, full)],
        scratch=[pltpu.VMEM((2, full, full), f32), pltpu.VMEM((modes, 2, full, full), f32)],
        flops=5_000_000_000,
        moved=12_000_000,
        limit=24,
    )(offsets.reshape(2), counts.reshape(1), *own, *right, *lower, probe, measured, table, order)

    near_pairs = [(2 * x + c, 2 * ((x ^ 1) if c == 0 else 3 - x) + c) for x in range(4) for c in range(2)]
    far_pairs = [(2 * x + c, 2 * (3 - x if c == 0 else (x ^ 1)) + c) for x in range(4) for c in range(2)]
    half_shape = (2, *block_shape[1:])
    summed = []
    theirs = [lax.ppermute(peer, "core", [(0, 1), (1, 0)]) for peer in (peer_re, peer_im)]
    for mine, other in zip((mine_re, mine_im), theirs):
        send, keep = call(
            cores_kernel, "add_cores", [vmem] * 2, [shaped(*half_shape)] * 2, moved=3_000_000
        )(mine, other)
        summed.append((keep, lax.ppermute(send, ("x", "core"), near_pairs)))
    from_left = passed_along(moves, cols, 1)
    arrived = []
    for keep, got in summed:
        arrived += [keep, got, lax.ppermute(keep[1] + got[1], ("x", "core"), far_pairs)]
    packed = call(columns_kernel, "add_columns", [vmem] * 6, [shaped(8, strip, 768)], moved=2_000_000)(*arrived)
    stays, _ = lax.optimization_barrier((stays, packed))
    down, held = call(down_kernel, "down", [smem, vmem, vmem], [shaped(2, full, full)] * 2, moved=2_000_000)(
        offsets.reshape(2), stays, from_left
    )
    from_above = passed_along(down, rows, 1)
    parts = lax.all_to_all(packed, "y", 0, 0, tiled=True)
    packed = call(depth_kernel, "add_depth", [vmem], [shaped(8, 8, 192)], moved=500_000)(parts)
    parts = lax.all_to_all(packed, ("z_lo", "z_hi"), 0, 0, tiled=True)
    share = jnp.sum(parts, axis=0).reshape(8, 2, modes, strip).transpose(1, 2, 3, 0)
    probe_new = own_probe - (512.0 ** -0.5) * share

    object_new = object_field - object_rate * (held + from_above)
    return (object_new, probe_new)


def solution(mesh):
    grid = jax.sharding.Mesh(mesh.devices.reshape(4, 4, 2, 8, 2), ("z_lo", "x", "z_hi", "y", "core"))
    rows = ("z_lo", "x")
    cols = ("z_hi", "y", "core")
    in_specs = (
        P(None, rows, cols),
        P(),
        P(rows, cols, None, None),
        P(rows, cols),
        P(rows, cols, None, None, None),
    )
    out_specs = (P(None, rows, cols), P(None, None, rows, cols))
    return jax.shard_map(local, mesh=grid, in_specs=in_specs, out_specs=out_specs, check_vma=False)
```

```python
import functools
import math

import jax
import jax.numpy as jnp
import ml_dtypes
import numpy as np
from jax import lax
from jax.experimental import pallas as pl
from jax.experimental.pallas import tpu as pltpu
from jax.sharding import PartitionSpec as P

object_rate = 0.25
f32 = jnp.float32
bf16 = jnp.bfloat16
half = 128
full = 256
modes = 6
strip = 16


def passed_along(x, axis, by):
    devices = lax.axis_size(axis)
    pairs = [(i, i + by) for i in range(devices) if 0 <= i + by < devices]
    return lax.ppermute(x, axis, pairs)


def halves_tables():
    place = np.arange(half)[:, None]
    freq = np.arange(half)[None, :]
    columns = column_order()[:half]
    tables = []
    for places in (place, columns[:, None]):
        for odd in (0, 1):
            angle = -2.0 * math.pi * ((places * (2 * freq + odd)) % full) / full
            re, im = np.cos(angle) / 16.0, np.sin(angle) / 16.0
            real_form = np.block([[re, im], [-im, re]]).astype(np.float32)
            for form in (real_form, real_form.T):
                high = form.astype(ml_dtypes.bfloat16)
                low = (form - high.astype(np.float32)).astype(ml_dtypes.bfloat16)
                tables.append(np.stack([high, low]))
    frequencies = np.zeros((full, full), np.float32)
    shuffle = np.zeros((full, full), np.float32)
    for k in range(full):
        frequencies[(k % 2) * half + k // 2, k] = 1.0
    shuffle[column_order(), np.arange(full)] = 1.0
    orders = np.stack([frequencies, frequencies.T, shuffle, shuffle.T])
    return np.stack(tables), orders.astype(ml_dtypes.bfloat16)


def column_order():
    columns = np.arange(full).reshape(2, 8, 2, 8)
    return columns.transpose(0, 2, 1, 3).reshape(-1)


def split(x):
    high = x.astype(bf16)
    return high, (x - high.astype(f32)).astype(bf16)


def dot(a, b):
    return jnp.dot(a, b, preferred_element_type=f32)


def data_by_table(high, low, table_ref, which):
    table_high, table_low = table_ref[which, 0], table_ref[which, 1]
    return dot(high, table_high) + (dot(high, table_low) + dot(low, table_high))


def table_by_data(table_ref, which, high, low):
    table_high, table_low = table_ref[which, 0], table_ref[which, 1]
    return dot(table_high, high) + (dot(table_low, high) + dot(table_high, low))


def put(high_ref, low_ref, index, at, left, right):
    high, low = split(jnp.concatenate([left, right], axis=1))
    high_ref[index, at : at + strip] = high
    low_ref[index, at : at + strip] = low


def beside(products, strips):
    count = len(products)
    for i, product in enumerate(products):
        product()
        for work in strips[i * len(strips) // count : (i + 1) * len(strips) // count]:
            work()


def step_stages(mode, core, refs):
    (probe_ref, window_ref, table_ref, a_high, a_low, b_high, b_low, mid_ref, near_ref, far_ref, sum_ref, obj_ref,
     mine_re_ref, mine_im_ref, peer_re_ref, peer_im_ref) = refs
    p = 2 * (mode % 2)

    def exits(r):
        at = slice(r, r + strip)
        probe_re, probe_im = probe_ref[0, mode, at].astype(f32), probe_ref[1, mode, at].astype(f32)
        win_re, win_im = window_ref[0, at], window_ref[1, at]
        re = probe_re * win_re - probe_im * win_im
        im = probe_re * win_im + probe_im * win_re
        put(a_high, a_low, p, r, re[:, :half] + re[:, half:], im[:, :half] + im[:, half:])
        put(a_high, a_low, p + 1, r, re[:, :half] - re[:, half:], im[:, :half] - im[:, half:])

    def far_columns(odd):
        mid_ref[p + odd] = data_by_table(a_high[p + odd], a_low[p + odd], table_ref, 4 + 2 * odd)

    def folds(r):
        even_top, even_bottom = mid_ref[p, r : r + strip], mid_ref[p, half + r : half + r + strip]
        odd_top, odd_bottom = mid_ref[p + 1, r : r + strip], mid_ref[p + 1, half + r : half + r + strip]
        for odd, even_fold, odd_fold in (
            (0, even_top + even_bottom, odd_top + odd_bottom),
            (1, even_top - even_bottom, odd_top - odd_bottom),
        ):
            put(b_high, b_low, p + odd, r, even_fold[:, :half], odd_fold[:, :half])
            put(b_high, b_low, p + odd, half + r, even_fold[:, half:], odd_fold[:, half:])

    def far_rows(odd):
        far_ref[mode, odd] = table_by_data(table_ref, 1 + 2 * odd, b_high[p + odd], b_low[p + odd])

    def sums(odd, r):
        re, im = far_ref[mode, odd, r : r + strip], far_ref[mode, odd, half + r : half + r + strip]
        sum_ref[odd, r : r + strip] += re * re + im * im

    def scale(odd, r):
        residual = sum_ref[odd, r : r + strip]
        for at in (r, half + r):
            scaled = far_ref[mode, odd, at : at + strip] * residual
            put(b_high, b_low, p + odd, at, scaled[:, :half], scaled[:, half:])

    def near_rows(odd):
        mid_ref[p + odd] = table_by_data(table_ref, 2 * odd, b_high[p + odd], b_low[p + odd])

    def unfolds(r):
        even_re, even_im = mid_ref[p, r : r + strip], mid_ref[p, half + r : half + r + strip]
        odd_re, odd_im = mid_ref[p + 1, r : r + strip], mid_ref[p + 1, half + r : half + r + strip]
        for at, re, im in ((r, even_re + odd_re, even_im + odd_im), (half + r, even_re - odd_re, even_im - odd_im)):
            put(a_high, a_low, p, at, re[:, :half], im[:, :half])
            put(a_high, a_low, p + 1, at, re[:, half:], im[:, half:])

    def near_columns(odd):
        near_ref[p + odd] = data_by_table(a_high[p + odd], a_low[p + odd], table_ref, 5 + 2 * odd)

    def grads(r):
        gradients(
            mode, r, core, probe_ref, window_ref, near_ref, obj_ref, mine_re_ref, mine_im_ref, peer_re_ref, peer_im_ref
        )

    both = range(2)
    long, short = range(0, full, strip), range(0, half, strip)
    ahead = (
        [functools.partial(exits, r) for r in long],
        [functools.partial(far_columns, odd) for odd in both],
        [functools.partial(folds, r) for r in short],
        [functools.partial(far_rows, odd) for odd in both],
        [functools.partial(sums, odd, r) for odd in both for r in short],
    )
    back = (
        [functools.partial(scale, odd, r) for odd in both for r in short],
        [functools.partial(near_rows, odd) for odd in both],
        [functools.partial(unfolds, r) for r in short],
        [functools.partial(near_columns, odd) for odd in both],
        [functools.partial(grads, r) for r in long],
    )
    return ahead, back


def pipelined(stages):
    none = ([], [], [], [], [])
    item = lambda i: stages[i] if 0 <= i < len(stages) else none
    for work in item(0)[0]:
        work()
    beside(item(0)[1], item(1)[0])
    for i in range(len(stages)):
        beside(item(i + 1)[1] or [lambda: None], item(i)[2])
        beside(item(i)[3], item(i - 1)[4] + item(i + 2)[0])
    for work in item(len(stages) - 1)[4]:
        work()


def reorder(x, order):
    high = x.astype(bf16)
    left = x - high.astype(f32)
    mid = left.astype(bf16)
    low = (left - mid.astype(f32)).astype(bf16)
    return dot(jnp.concatenate([high, mid, low], axis=1), jnp.concatenate([order, order, order], axis=0))


def store_strip(mine_ref, peer_ref, mode, r, left, right, core):
    z, x = r // strip // 4, r // strip % 4
    lanes = lax.broadcasted_iota(jnp.int32, (strip, half), 1)
    first = jnp.where(lanes < half // 2, left, pltpu.roll(right, half // 2, 1))
    second = jnp.where(lanes < half // 2, pltpu.roll(left, half // 2, 1), right)
    mine_ref[x, z, mode] = jnp.where(core == 0, first, second)
    peer_ref[x, z, mode] = jnp.where(core == 0, second, first)


def gradients(mode, r, core, probe_ref, window_ref, mid_ref, obj_ref, mine_re_ref, mine_im_ref, peer_re_ref, peer_im_ref):
    a = 2 * (mode % 2)
    at = slice(r, r + strip)
    even, odd = mid_ref[a, at], mid_ref[a + 1, at]
    up, down = even + odd, even - odd
    parts_re, parts_im = [], []
    for side, near in enumerate((up, down)):
        lanes = slice(side * half, side * half + half)
        near_re, near_im = near[:, :half], near[:, half:]
        probe_re, probe_im = probe_ref[0, mode, at, lanes].astype(f32), probe_ref[1, mode, at, lanes].astype(f32)
        win_re, win_im = window_ref[0, at, lanes], window_ref[1, at, lanes]
        parts_re.append(win_re * near_re + win_im * near_im)
        parts_im.append(win_re * near_im - win_im * near_re)
        obj_re = probe_re * near_re + probe_im * near_im
        obj_im = probe_re * near_im - probe_im * near_re
        if mode:
            obj_re = obj_re + obj_ref[0, at, lanes]
            obj_im = obj_im + obj_ref[1, at, lanes]
        obj_ref[0, at, lanes] = obj_re
        obj_ref[1, at, lanes] = obj_im
    store_strip(mine_re_ref, peer_re_ref, mode, r, *parts_re, core)
    store_strip(mine_im_ref, peer_im_ref, mode, r, *parts_im, core)


def cells():
    rows = lax.broadcasted_iota(jnp.int32, (full, full), 0)
    cols = lax.broadcasted_iota(jnp.int32, (full, full), 1)
    return rows, cols


def prepare_kernel(
    probe_in, intensity_in, table_in, order_in, probe_out, measured_out, table_out, order_out,
    probe_ref, intensity_ref, order_ref, sems,
):
    copies = [
        pltpu.make_async_copy(source, target, sems.at[i])
        for i, (source, target) in enumerate(
            [(order_in, order_ref), (intensity_in, intensity_ref), (probe_in, probe_ref), (table_in, table_out)]
        )
    ]
    for copy in copies:
        copy.start()
    copies[0].wait()
    copies[1].wait()
    frequencies, turned, shuffle = order_ref[0], order_ref[1], order_ref[2]
    measured_out[...] = dot(dot(frequencies, intensity_ref[...]).astype(bf16), turned)
    order_out[0] = shuffle
    order_out[1] = order_ref[3]
    copies[2].wait()
    for part in range(2):
        for mode in range(modes):
            probe_out[part, mode] = dot(probe_ref[part, mode], shuffle).astype(bf16)
    copies[3].wait()


def main_kernel(
    offset_ref, count_ref, own_re, own_im, right_re, right_im, lower_re, lower_im, probe_ref, measured_ref,
    table_ref, order_ref, mine_re_ref, mine_im_ref, peer_re_ref, peer_im_ref, stays_ref, moves_ref,
    window_ref, far_ref, a_high, a_low, b_high, b_low, mid_ref, near_ref, sum_ref, obj_ref,
):
    row_offset = offset_ref[0]
    col_offset = offset_ref[1]
    live = (count_ref[0] > 0).astype(f32)
    core = lax.axis_index("core")
    rows, cols = cells()
    in_row = rows >= row_offset
    in_col = cols >= col_offset
    parts = ((own_re, right_re, lower_re), (own_im, right_im, lower_im))
    for part, (own_ref, right_ref, lower_ref) in enumerate(parts):
        mixed = jnp.where(in_row, jnp.where(in_col, own_ref[...], right_ref[...]), lower_ref[...])
        mixed = pltpu.roll(mixed, lax.rem(full - row_offset, full), 0)
        window_ref[part] = reorder(pltpu.roll(mixed, lax.rem(full - col_offset, full), 1), order_ref[0])
    sum_ref[0] = -measured_ref[:half]
    sum_ref[1] = -measured_ref[half:]
    refs = (
        probe_ref, window_ref, table_ref, a_high, a_low, b_high, b_low, mid_ref, near_ref, far_ref, sum_ref, obj_ref,
        mine_re_ref, mine_im_ref, peer_re_ref, peer_im_ref,
    )
    stages = [step_stages(mode, core, refs) for mode in range(modes)]
    pipelined([ahead for ahead, back in stages])
    sum_ref[...] = sum_ref[...] * live
    pipelined([back for ahead, back in stages])
    for part in range(2):
        placed = reorder(obj_ref[part], order_ref[1])
        placed = pltpu.roll(pltpu.roll(placed, row_offset, 0), col_offset, 1)
        stays_ref[part] = jnp.where(in_col, placed, 0.0)
        moves_ref[part, :full] = jnp.where(in_col, 0.0, placed)
        moves_ref[part, full:] = jnp.zeros((8, full), f32) + row_offset.astype(f32)


def mix_kernel(offset_ref, own_ref, right_ref, out_ref):
    rows, cols = cells()
    out_ref[...] = jnp.where(cols >= offset_ref[1], own_ref[...], right_ref[...])


def down_kernel(offset_ref, stays_ref, moved_ref, down_ref, held_ref):
    rows, cols = cells()
    in_row = rows >= offset_ref[0]
    left_in_row = rows.astype(f32) >= moved_ref[0, full : full + 1]
    for part in range(2):
        stays, moved = stays_ref[part], moved_ref[part, :full]
        down_ref[part] = jnp.where(in_row, 0.0, stays) + jnp.where(left_in_row, 0.0, moved)
        held_ref[part] = jnp.where(in_row, stays, 0.0) + jnp.where(left_in_row, moved, 0.0)


def cores_kernel(mine_ref, theirs_ref, send_ref, keep_ref):
    x = lax.axis_index("x")
    core = lax.axis_index("core")
    first = jnp.where(core == 0, x ^ 1, 3 - x)
    second = jnp.where(core == 0, 3 - x, x ^ 1)
    for ref, slot, index in ((send_ref, 0, first), (send_ref, 1, x ^ 2), (keep_ref, 0, x), (keep_ref, 1, second)):
        ref[slot] = mine_ref[index] + theirs_ref[index]


def columns_kernel(kept_re, got_re, came_re, kept_im, got_im, came_im, out_ref):
    for part, (kept_ref, got_ref, came_ref) in enumerate(((kept_re, got_re, came_re), (kept_im, got_im, came_im))):
        for z in range(4):
            turned = (kept_ref[0, z] + got_ref[0, z] + came_ref[z]).reshape(96, half).T
            lane = z * 192 + part * 96
            for y in range(8):
                for z_hi in range(2):
                    at = z_hi * 64 + y * 8
                    out_ref[y, z_hi * 8 : z_hi * 8 + 8, lane : lane + 96] = turned[at : at + 8]


def depth_kernel(parts_ref, out_ref):
    total = parts_ref[0]
    for i in range(1, 8):
        total = total + parts_ref[i]
    for z in range(4):
        for z_hi in range(2):
            out_ref[2 * z + z_hi] = total[z_hi * 8 : z_hi * 8 + 8, z * 192 : z * 192 + 192]


def shaped(*shape, dtype=f32):
    return jax.ShapeDtypeStruct(shape, dtype)


step_scratch = [pltpu.VMEM((4, full, full), bf16)] * 4 + [
    pltpu.VMEM((4, full, full), f32),
    pltpu.VMEM((4, full, full), f32),
    pltpu.VMEM((2, half, full), f32),
    pltpu.VMEM((2, full, full), f32),
]
vmem = pl.BlockSpec(memory_space=pltpu.VMEM)
smem = pl.BlockSpec(memory_space=pltpu.SMEM)


def call(kernel, name, inputs, outputs, scratch=(), flops=0, moved=0, limit=16):
    return pl.pallas_call(
        kernel,
        out_shape=tuple(outputs) if len(outputs) > 1 else outputs[0],
        in_specs=inputs,
        out_specs=(vmem,) * len(outputs) if len(outputs) > 1 else vmem,
        scratch_shapes=scratch,
        compiler_params=pltpu.CompilerParams(vmem_limit_bytes=limit * 1024 * 1024),
        cost_estimate=pl.CostEstimate(flops=flops, bytes_accessed=moved, transcendentals=0),
        name=name,
    )


def local(object_field, probe_modes, offsets, counts, intensity):
    rows = ("z_lo", "x")
    cols = ("z_hi", "y", "core")
    tables, orders = halves_tables()
    above_offset = passed_along(offsets, rows, 1).reshape(2)
    own = (object_field[0], object_field[1])
    above_offset, own_im = lax.optimization_barrier((above_offset, own[1]))
    own = (own[0], own_im)
    right = [passed_along(part, cols, -1) for part in own]
    lower = []
    for part, beside in zip(own, right):
        mixed = call(mix_kernel, "mix", [smem, vmem, vmem], [shaped(full, full)], moved=1_000_000)(
            above_offset, part, beside
        )
        lower.append(passed_along(mixed, rows, -1))
    start = (0, 0, lax.axis_index(rows) * strip, lax.axis_index(cols) * 8)
    own_probe = lax.dynamic_slice(probe_modes, start, (2, modes, strip, 8)).astype(f32)
    probe, measured, table, order = call(
        prepare_kernel,
        "prepare",
        [pl.BlockSpec(memory_space=pl.ANY)] * 4,
        [
            shaped(2, modes, full, full, dtype=bf16),
            shaped(full, full),
            shaped(8, 2, full, full, dtype=bf16),
            shaped(2, full, full, dtype=bf16),
        ],
        scratch=[
            pltpu.VMEM((2, modes, full, full), bf16),
            pltpu.VMEM((full, full), bf16),
            pltpu.VMEM((4, full, full), bf16),
            pltpu.SemaphoreType.DMA((4,)),
        ],
        flops=500_000_000,
        moved=8_000_000,
    )(probe_modes, intensity[0, 0, 0], jnp.asarray(tables), jnp.asarray(orders))
    block_shape = (4, 4, modes, strip, half)
    mine_re, mine_im, peer_re, peer_im, stays, moves = call(
        main_kernel,
        "step",
        [smem, smem] + [vmem] * 10,
        [shaped(*block_shape)] * 4 + [shaped(2, full, full), shaped(2, full + 8, full)],
        scratch=[pltpu.VMEM((2, full, full), f32), pltpu.VMEM((modes, 2, full, full), f32), *step_scratch],
        flops=5_000_000_000,
        moved=12_000_000,
        limit=24,
    )(offsets.reshape(2), counts.reshape(1), *own, *right, *lower, probe, measured, table, order)

    near_pairs = [(2 * x + c, 2 * ((x ^ 1) if c == 0 else 3 - x) + c) for x in range(4) for c in range(2)]
    far_pairs = [(2 * x + c, 2 * (3 - x if c == 0 else (x ^ 1)) + c) for x in range(4) for c in range(2)]
    half_shape = (2, *block_shape[1:])
    summed = []
    theirs = [lax.ppermute(peer, "core", [(0, 1), (1, 0)]) for peer in (peer_re, peer_im)]
    for mine, other in zip((mine_re, mine_im), theirs):
        send, keep = call(
            cores_kernel, "add_cores", [vmem] * 2, [shaped(*half_shape)] * 2, moved=3_000_000
        )(mine, other)
        summed.append((keep, lax.ppermute(send, ("x", "core"), near_pairs)))
    from_left = passed_along(moves, cols, 1)
    arrived = []
    for keep, got in summed:
        arrived += [keep, got, lax.ppermute(keep[1] + got[1], ("x", "core"), far_pairs)]
    packed = call(columns_kernel, "add_columns", [vmem] * 6, [shaped(8, strip, 768)], moved=2_000_000)(*arrived)
    stays, _ = lax.optimization_barrier((stays, packed))
    down, held = call(down_kernel, "down", [smem, vmem, vmem], [shaped(2, full, full)] * 2, moved=2_000_000)(
        offsets.reshape(2), stays, from_left
    )
    from_above = passed_along(down, rows, 1)
    parts = lax.all_to_all(packed, "y", 0, 0, tiled=True)
    packed = call(depth_kernel, "add_depth", [vmem], [shaped(8, 8, 192)], moved=500_000)(parts)
    parts = lax.all_to_all(packed, ("z_lo", "z_hi"), 0, 0, tiled=True)
    share = jnp.sum(parts, axis=0).reshape(8, 2, modes, strip).transpose(1, 2, 3, 0)
    probe_new = own_probe - (512.0 ** -0.5) * share

    object_new = object_field - object_rate * (held + from_above)
    return (object_new, probe_new)


def solution(mesh):
    grid = jax.sharding.Mesh(mesh.devices.reshape(4, 4, 2, 8, 2), ("z_lo", "x", "z_hi", "y", "core"))
    rows = ("z_lo", "x")
    cols = ("z_hi", "y", "core")
    in_specs = (
        P(None, rows, cols),
        P(),
        P(rows, cols, None, None),
        P(rows, cols),
        P(rows, cols, None, None, None),
    )
    out_specs = (P(None, rows, cols), P(None, None, rows, cols))
    return jax.shard_map(local, mesh=grid, in_specs=in_specs, out_specs=out_specs, check_vma=False)
```

```python
import functools
import math

import jax
import jax.numpy as jnp
import ml_dtypes
import numpy as np
from jax import lax
from jax.experimental import pallas as pl
from jax.experimental.pallas import tpu as pltpu
from jax.sharding import PartitionSpec as P

object_rate = 0.25
f32 = jnp.float32
bf16 = jnp.bfloat16
half = 128
full = 256
modes = 6
strip = 16


def passed_along(x, axis, by):
    devices = lax.axis_size(axis)
    pairs = [(i, i + by) for i in range(devices) if 0 <= i + by < devices]
    return lax.ppermute(x, axis, pairs)


def halves_tables():
    place = np.arange(half)[:, None]
    freq = np.arange(half)[None, :]
    columns = column_order()[:half]
    tables = []
    for places in (place, columns[:, None]):
        for odd in (0, 1):
            angle = -2.0 * math.pi * ((places * (2 * freq + odd)) % full) / full
            re, im = np.cos(angle) / 16.0, np.sin(angle) / 16.0
            real_form = np.block([[re, im], [-im, re]]).astype(np.float32)
            for form in (real_form, real_form.T):
                high = form.astype(ml_dtypes.bfloat16)
                low = (form - high.astype(np.float32)).astype(ml_dtypes.bfloat16)
                tables.append(np.stack([high, low]))
    frequencies = np.zeros((full, full), np.float32)
    shuffle = np.zeros((full, full), np.float32)
    for k in range(full):
        frequencies[(k % 2) * half + k // 2, k] = 1.0
    shuffle[column_order(), np.arange(full)] = 1.0
    orders = np.stack([frequencies, frequencies.T, shuffle, shuffle.T])
    return np.stack(tables), orders.astype(ml_dtypes.bfloat16)


def column_order():
    columns = np.arange(full).reshape(2, 8, 2, 8)
    return columns.transpose(0, 2, 1, 3).reshape(-1)


def split(x):
    high = x.astype(bf16)
    return high, (x - high.astype(f32)).astype(bf16)


def dot(a, b):
    return jnp.dot(a, b, preferred_element_type=f32)


def data_by_table(high, low, table_ref, which):
    table_high, table_low = table_ref[which, 0], table_ref[which, 1]
    return dot(high, table_high) + (dot(high, table_low) + dot(low, table_high))


def table_by_data(table_ref, which, high, low):
    table_high, table_low = table_ref[which, 0], table_ref[which, 1]
    return dot(table_high, high) + (dot(table_low, high) + dot(table_high, low))


def put(high_ref, low_ref, index, at, left, right):
    high, low = split(jnp.concatenate([left, right], axis=1))
    high_ref[index, at : at + strip] = high
    low_ref[index, at : at + strip] = low


def beside(products, strips):
    count = len(products)
    for i, product in enumerate(products):
        product()
        for work in strips[i * len(strips) // count : (i + 1) * len(strips) // count]:
            work()


def step_stages(mode, core, refs):
    (probe_ref, window_ref, table_ref, a_high, a_low, b_high, b_low, mid_ref, near_ref, far_ref, sum_ref, obj_ref,
     mine_re_ref, mine_im_ref, peer_re_ref, peer_im_ref) = refs
    p = 2 * (mode % 2)

    def exits(r):
        at = slice(r, r + strip)
        probe_re, probe_im = probe_ref[0, mode, at].astype(f32), probe_ref[1, mode, at].astype(f32)
        win_re, win_im = window_ref[0, at], window_ref[1, at]
        re = probe_re * win_re - probe_im * win_im
        im = probe_re * win_im + probe_im * win_re
        put(a_high, a_low, p, r, re[:, :half] + re[:, half:], im[:, :half] + im[:, half:])
        put(a_high, a_low, p + 1, r, re[:, :half] - re[:, half:], im[:, :half] - im[:, half:])

    def far_columns(odd):
        mid_ref[p + odd] = data_by_table(a_high[p + odd], a_low[p + odd], table_ref, 4 + 2 * odd)

    def folds(r):
        even_top, even_bottom = mid_ref[p, r : r + strip], mid_ref[p, half + r : half + r + strip]
        odd_top, odd_bottom = mid_ref[p + 1, r : r + strip], mid_ref[p + 1, half + r : half + r + strip]
        for odd, even_fold, odd_fold in (
            (0, even_top + even_bottom, odd_top + odd_bottom),
            (1, even_top - even_bottom, odd_top - odd_bottom),
        ):
            put(b_high, b_low, p + odd, r, even_fold[:, :half], odd_fold[:, :half])
            put(b_high, b_low, p + odd, half + r, even_fold[:, half:], odd_fold[:, half:])

    def far_rows(odd):
        far_ref[mode, odd] = table_by_data(table_ref, 1 + 2 * odd, b_high[p + odd], b_low[p + odd])

    def sums(odd, r):
        re, im = far_ref[mode, odd, r : r + strip], far_ref[mode, odd, half + r : half + r + strip]
        sum_ref[odd, r : r + strip] += re * re + im * im

    def scale(odd, r):
        residual = sum_ref[odd, r : r + strip]
        for at in (r, half + r):
            scaled = far_ref[mode, odd, at : at + strip] * residual
            put(b_high, b_low, p + odd, at, scaled[:, :half], scaled[:, half:])

    def near_rows(odd):
        mid_ref[p + odd] = table_by_data(table_ref, 2 * odd, b_high[p + odd], b_low[p + odd])

    def unfolds(r):
        even_re, even_im = mid_ref[p, r : r + strip], mid_ref[p, half + r : half + r + strip]
        odd_re, odd_im = mid_ref[p + 1, r : r + strip], mid_ref[p + 1, half + r : half + r + strip]
        for at, re, im in ((r, even_re + odd_re, even_im + odd_im), (half + r, even_re - odd_re, even_im - odd_im)):
            put(a_high, a_low, p, at, re[:, :half], im[:, :half])
            put(a_high, a_low, p + 1, at, re[:, half:], im[:, half:])

    def near_columns(odd):
        near_ref[p + odd] = data_by_table(a_high[p + odd], a_low[p + odd], table_ref, 5 + 2 * odd)

    def grads(r):
        gradients(
            mode, r, core, probe_ref, window_ref, near_ref, obj_ref, mine_re_ref, mine_im_ref, peer_re_ref, peer_im_ref
        )

    both = range(2)
    long, short = range(0, full, strip), range(0, half, strip)
    ahead = (
        [functools.partial(exits, r) for r in long],
        [functools.partial(far_columns, odd) for odd in both],
        [functools.partial(folds, r) for r in short],
        [functools.partial(far_rows, odd) for odd in both],
        [functools.partial(sums, odd, r) for odd in both for r in short],
    )
    back = (
        [functools.partial(scale, odd, r) for odd in both for r in short],
        [functools.partial(near_rows, odd) for odd in both],
        [functools.partial(unfolds, r) for r in short],
        [functools.partial(near_columns, odd) for odd in both],
        [functools.partial(grads, r) for r in long],
    )
    return ahead, back


def pipelined(stages):
    none = ([], [], [], [], [])
    item = lambda i: stages[i] if 0 <= i < len(stages) else none
    for work in item(0)[0]:
        work()
    beside(item(0)[1], item(1)[0])
    for i in range(len(stages)):
        beside(item(i + 1)[1] or [lambda: None], item(i)[2])
        beside(item(i)[3], item(i - 1)[4] + item(i + 2)[0])
    for work in item(len(stages) - 1)[4]:
        work()


def reorder(x, order):
    high = x.astype(bf16)
    left = x - high.astype(f32)
    mid = left.astype(bf16)
    low = (left - mid.astype(f32)).astype(bf16)
    return dot(jnp.concatenate([high, mid, low], axis=1), jnp.concatenate([order, order, order], axis=0))


def store_strip(mine_ref, peer_ref, mode, r, left, right, core):
    z, x = r // strip // 4, r // strip % 4
    lanes = lax.broadcasted_iota(jnp.int32, (strip, half), 1)
    first = jnp.where(lanes < half // 2, left, pltpu.roll(right, half // 2, 1))
    second = jnp.where(lanes < half // 2, pltpu.roll(left, half // 2, 1), right)
    mine_ref[x, z, mode] = jnp.where(core == 0, first, second)
    peer_ref[x, z, mode] = jnp.where(core == 0, second, first)


def gradients(mode, r, core, probe_ref, window_ref, mid_ref, obj_ref, mine_re_ref, mine_im_ref, peer_re_ref, peer_im_ref):
    a = 2 * (mode % 2)
    at = slice(r, r + strip)
    even, odd = mid_ref[a, at], mid_ref[a + 1, at]
    up, down = even + odd, even - odd
    parts_re, parts_im = [], []
    for side, near in enumerate((up, down)):
        lanes = slice(side * half, side * half + half)
        near_re, near_im = near[:, :half], near[:, half:]
        probe_re, probe_im = probe_ref[0, mode, at, lanes].astype(f32), probe_ref[1, mode, at, lanes].astype(f32)
        win_re, win_im = window_ref[0, at, lanes], window_ref[1, at, lanes]
        parts_re.append(win_re * near_re + win_im * near_im)
        parts_im.append(win_re * near_im - win_im * near_re)
        obj_re = probe_re * near_re + probe_im * near_im
        obj_im = probe_re * near_im - probe_im * near_re
        if mode:
            obj_re = obj_re + obj_ref[0, at, lanes]
            obj_im = obj_im + obj_ref[1, at, lanes]
        obj_ref[0, at, lanes] = obj_re
        obj_ref[1, at, lanes] = obj_im
    store_strip(mine_re_ref, peer_re_ref, mode, r, *parts_re, core)
    store_strip(mine_im_ref, peer_im_ref, mode, r, *parts_im, core)


def cells():
    rows = lax.broadcasted_iota(jnp.int32, (full, full), 0)
    cols = lax.broadcasted_iota(jnp.int32, (full, full), 1)
    return rows, cols


def prepare_kernel(
    probe_in, intensity_in, table_in, order_in, probe_out, measured_out, table_out, order_out,
    probe_ref, intensity_ref, order_ref, sems,
):
    copies = [
        pltpu.make_async_copy(source, target, sems.at[i])
        for i, (source, target) in enumerate(
            [(order_in, order_ref), (intensity_in, intensity_ref), (probe_in, probe_ref), (table_in, table_out)]
        )
    ]
    for copy in copies:
        copy.start()
    copies[0].wait()
    copies[1].wait()
    frequencies, turned, shuffle = order_ref[0], order_ref[1], order_ref[2]
    measured_out[...] = dot(dot(frequencies, intensity_ref[...]).astype(bf16), turned)
    order_out[0] = shuffle
    order_out[1] = order_ref[3]
    copies[2].wait()
    for part in range(2):
        for mode in range(modes):
            probe_out[part, mode] = dot(probe_ref[part, mode], shuffle).astype(bf16)
    copies[3].wait()


def main_kernel(
    offset_ref, count_ref, own_ref, right_ref, lower_ref, probe_ref, measured_ref,
    table_ref, order_ref, mine_re_ref, mine_im_ref, peer_re_ref, peer_im_ref, stays_ref, moves_ref,
    window_ref, far_ref, a_high, a_low, b_high, b_low, mid_ref, near_ref, sum_ref, obj_ref,
):
    row_offset = offset_ref[0]
    col_offset = offset_ref[1]
    live = (count_ref[0] > 0).astype(f32)
    core = lax.axis_index("core")
    rows, cols = cells()
    in_row = rows >= row_offset
    in_col = cols >= col_offset
    for part in range(2):
        mixed = jnp.where(in_row, jnp.where(in_col, own_ref[part], right_ref[part]), lower_ref[part])
        mixed = pltpu.roll(mixed, lax.rem(full - row_offset, full), 0)
        window_ref[part] = reorder(pltpu.roll(mixed, lax.rem(full - col_offset, full), 1), order_ref[0])
    sum_ref[0] = -measured_ref[:half]
    sum_ref[1] = -measured_ref[half:]
    refs = (
        probe_ref, window_ref, table_ref, a_high, a_low, b_high, b_low, mid_ref, near_ref, far_ref, sum_ref, obj_ref,
        mine_re_ref, mine_im_ref, peer_re_ref, peer_im_ref,
    )
    stages = [step_stages(mode, core, refs) for mode in range(modes)]
    pipelined([ahead for ahead, back in stages])
    sum_ref[...] = sum_ref[...] * live
    pipelined([back for ahead, back in stages])
    for part in range(2):
        placed = reorder(obj_ref[part], order_ref[1])
        placed = pltpu.roll(pltpu.roll(placed, row_offset, 0), col_offset, 1)
        stays_ref[part] = jnp.where(in_col, placed, 0.0)
        moves_ref[part, :full] = jnp.where(in_col, 0.0, placed)
        moves_ref[part, full:] = jnp.zeros((8, full), f32) + row_offset.astype(f32)


def hold_kernel(tile_in, tile_out, sem):
    copy = pltpu.make_async_copy(tile_in, tile_out, sem)
    copy.start()
    copy.wait()


def mix_kernel(offset_ref, own_ref, right_ref, out_ref):
    rows, cols = cells()
    in_col = cols >= offset_ref[1]
    for part in range(2):
        out_ref[part] = jnp.where(in_col, own_ref[part], right_ref[part])


def down_kernel(offset_ref, stays_ref, moved_ref, down_ref, held_ref):
    rows, cols = cells()
    in_row = rows >= offset_ref[0]
    left_in_row = rows.astype(f32) >= moved_ref[0, full : full + 1]
    for part in range(2):
        stays, moved = stays_ref[part], moved_ref[part, :full]
        down_ref[part] = jnp.where(in_row, 0.0, stays) + jnp.where(left_in_row, 0.0, moved)
        held_ref[part] = jnp.where(in_row, stays, 0.0) + jnp.where(left_in_row, moved, 0.0)


def cores_kernel(mine_ref, theirs_ref, send_ref, keep_ref):
    x = lax.axis_index("x")
    core = lax.axis_index("core")
    first = jnp.where(core == 0, x ^ 1, 3 - x)
    second = jnp.where(core == 0, 3 - x, x ^ 1)
    for ref, slot, index in ((send_ref, 0, first), (send_ref, 1, x ^ 2), (keep_ref, 0, x), (keep_ref, 1, second)):
        ref[slot] = mine_ref[index] + theirs_ref[index]


def columns_kernel(kept_re, got_re, came_re, kept_im, got_im, came_im, out_ref):
    for part, (kept_ref, got_ref, came_ref) in enumerate(((kept_re, got_re, came_re), (kept_im, got_im, came_im))):
        for z in range(4):
            turned = (kept_ref[0, z] + got_ref[0, z] + came_ref[z]).reshape(96, half).T
            lane = z * 192 + part * 96
            for y in range(8):
                for z_hi in range(2):
                    at = z_hi * 64 + y * 8
                    out_ref[y, z_hi * 8 : z_hi * 8 + 8, lane : lane + 96] = turned[at : at + 8]


def depth_kernel(parts_ref, out_ref):
    total = parts_ref[0]
    for i in range(1, 8):
        total = total + parts_ref[i]
    for z in range(4):
        for z_hi in range(2):
            out_ref[2 * z + z_hi] = total[z_hi * 8 : z_hi * 8 + 8, z * 192 : z * 192 + 192]


def shaped(*shape, dtype=f32):
    return jax.ShapeDtypeStruct(shape, dtype)


step_scratch = [pltpu.VMEM((4, full, full), bf16)] * 4 + [
    pltpu.VMEM((4, full, full), f32),
    pltpu.VMEM((4, full, full), f32),
    pltpu.VMEM((2, half, full), f32),
    pltpu.VMEM((2, full, full), f32),
]
vmem = pl.BlockSpec(memory_space=pltpu.VMEM)
smem = pl.BlockSpec(memory_space=pltpu.SMEM)


def call(kernel, name, inputs, outputs, scratch=(), flops=0, moved=0, limit=4):
    return pl.pallas_call(
        kernel,
        out_shape=tuple(outputs) if len(outputs) > 1 else outputs[0],
        in_specs=inputs,
        out_specs=(vmem,) * len(outputs) if len(outputs) > 1 else vmem,
        scratch_shapes=scratch,
        compiler_params=pltpu.CompilerParams(vmem_limit_bytes=limit * 1024 * 1024),
        cost_estimate=pl.CostEstimate(flops=flops, bytes_accessed=moved, transcendentals=0),
        name=name,
    )


def local(object_field, probe_modes, offsets, counts, intensity):
    rows = ("z_lo", "x")
    cols = ("z_hi", "y", "core")
    tables, orders = halves_tables()
    right = passed_along(object_field, cols, -1)
    above_offset = passed_along(offsets, rows, 1).reshape(2)
    above_offset, tile = lax.optimization_barrier((above_offset, object_field))
    own = call(
        hold_kernel, "hold", [pl.BlockSpec(memory_space=pl.ANY)], [shaped(2, full, full)],
        scratch=[pltpu.SemaphoreType.DMA], moved=1_000_000,
    )(tile)
    mixed = call(mix_kernel, "mix", [smem, vmem, vmem], [shaped(2, full, full)], moved=2_000_000)(
        above_offset, own, right
    )
    lower = passed_along(mixed, rows, -1)
    start = (0, 0, lax.axis_index(rows) * strip, lax.axis_index(cols) * 8)
    own_probe = lax.dynamic_slice(probe_modes, start, (2, modes, strip, 8)).astype(f32)
    probe, measured, table, order = call(
        prepare_kernel,
        "prepare",
        [pl.BlockSpec(memory_space=pl.ANY)] * 4,
        [
            shaped(2, modes, full, full, dtype=bf16),
            shaped(full, full),
            shaped(8, 2, full, full, dtype=bf16),
            shaped(2, full, full, dtype=bf16),
        ],
        scratch=[
            pltpu.VMEM((2, modes, full, full), bf16),
            pltpu.VMEM((full, full), bf16),
            pltpu.VMEM((4, full, full), bf16),
            pltpu.SemaphoreType.DMA((4,)),
        ],
        flops=500_000_000,
        moved=8_000_000,
        limit=6,
    )(probe_modes, intensity[0, 0, 0], jnp.asarray(tables), jnp.asarray(orders))
    block_shape = (4, 4, modes, strip, half)
    mine_re, mine_im, peer_re, peer_im, stays, moves = call(
        main_kernel,
        "step",
        [smem, smem] + [vmem] * 7,
        [shaped(*block_shape)] * 4 + [shaped(2, full, full), shaped(2, full + 8, full)],
        scratch=[pltpu.VMEM((2, full, full), f32), pltpu.VMEM((modes, 2, full, full), f32), *step_scratch],
        flops=5_000_000_000,
        moved=12_000_000,
        limit=14,
    )(offsets.reshape(2), counts.reshape(1), own, right, lower, probe, measured, table, order)

    near_pairs = [(2 * x + c, 2 * ((x ^ 1) if c == 0 else 3 - x) + c) for x in range(4) for c in range(2)]
    far_pairs = [(2 * x + c, 2 * (3 - x if c == 0 else (x ^ 1)) + c) for x in range(4) for c in range(2)]
    half_shape = (2, *block_shape[1:])
    summed = []
    theirs = [lax.ppermute(peer, "core", [(0, 1), (1, 0)]) for peer in (peer_re, peer_im)]
    for mine, other in zip((mine_re, mine_im), theirs):
        send, keep = call(
            cores_kernel, "add_cores", [vmem] * 2, [shaped(*half_shape)] * 2, moved=3_000_000
        )(mine, other)
        summed.append((keep, lax.ppermute(send, ("x", "core"), near_pairs)))
    from_left = passed_along(moves, cols, 1)
    arrived = []
    for keep, got in summed:
        arrived += [keep, got, lax.ppermute(keep[1] + got[1], ("x", "core"), far_pairs)]
    packed = call(columns_kernel, "add_columns", [vmem] * 6, [shaped(8, strip, 768)], moved=2_000_000)(*arrived)
    stays, _ = lax.optimization_barrier((stays, packed))
    down, held = call(down_kernel, "down", [smem, vmem, vmem], [shaped(2, full, full)] * 2, moved=2_000_000)(
        offsets.reshape(2), stays, from_left
    )
    from_above = passed_along(down, rows, 1)
    parts = lax.all_to_all(packed, "y", 0, 0, tiled=True)
    packed = call(depth_kernel, "add_depth", [vmem], [shaped(8, 8, 192)], moved=500_000)(parts)
    parts = lax.all_to_all(packed, ("z_lo", "z_hi"), 0, 0, tiled=True)
    share = jnp.sum(parts, axis=0).reshape(8, 2, modes, strip).transpose(1, 2, 3, 0)
    probe_new = own_probe - (512.0 ** -0.5) * share

    object_new = object_field - object_rate * (held + from_above)
    return (object_new, probe_new)


def solution(mesh):
    grid = jax.sharding.Mesh(mesh.devices.reshape(4, 4, 2, 8, 2), ("z_lo", "x", "z_hi", "y", "core"))
    rows = ("z_lo", "x")
    cols = ("z_hi", "y", "core")
    in_specs = (
        P(None, rows, cols),
        P(),
        P(rows, cols, None, None),
        P(rows, cols),
        P(rows, cols, None, None, None),
    )
    out_specs = (P(None, rows, cols), P(None, None, rows, cols))
    return jax.shard_map(local, mesh=grid, in_specs=in_specs, out_specs=out_specs, check_vma=False)
```

```python
import functools
import math

import jax
import jax.numpy as jnp
import ml_dtypes
import numpy as np
from jax import lax
from jax.experimental import pallas as pl
from jax.experimental.pallas import tpu as pltpu
from jax.sharding import PartitionSpec as P

object_rate = 0.25
f32 = jnp.float32
bf16 = jnp.bfloat16
half = 128
full = 256
modes = 6
strip = 16


def passed_along(x, axis, by):
    devices = lax.axis_size(axis)
    pairs = [(i, i + by) for i in range(devices) if 0 <= i + by < devices]
    return lax.ppermute(x, axis, pairs)


def halves_tables():
    place = np.arange(half)[:, None]
    freq = np.arange(half)[None, :]
    columns = column_order()[:half]
    tables = []
    for places in (place, columns[:, None]):
        for odd in (0, 1):
            angle = -2.0 * math.pi * ((places * (2 * freq + odd)) % full) / full
            re, im = np.cos(angle) / 16.0, np.sin(angle) / 16.0
            real_form = np.block([[re, im], [-im, re]]).astype(np.float32)
            for form in (real_form, real_form.T):
                high = form.astype(ml_dtypes.bfloat16)
                low = (form - high.astype(np.float32)).astype(ml_dtypes.bfloat16)
                tables.append(np.stack([high, low]))
    frequencies = np.zeros((full, full), np.float32)
    shuffle = np.zeros((full, full), np.float32)
    for k in range(full):
        frequencies[(k % 2) * half + k // 2, k] = 1.0
    shuffle[column_order(), np.arange(full)] = 1.0
    orders = np.stack([frequencies, frequencies.T, shuffle, shuffle.T])
    return np.stack(tables), orders.astype(ml_dtypes.bfloat16)


def column_order():
    columns = np.arange(full).reshape(2, 8, 2, 8)
    return columns.transpose(0, 2, 1, 3).reshape(-1)


def split(x):
    high = x.astype(bf16)
    return high, (x - high.astype(f32)).astype(bf16)


def dot(a, b):
    return jnp.dot(a, b, preferred_element_type=f32)


def data_by_table(high, low, table_ref, which):
    table_high, table_low = table_ref[which, 0], table_ref[which, 1]
    return dot(high, table_high) + (dot(high, table_low) + dot(low, table_high))


def table_by_data(table_ref, which, high, low):
    table_high, table_low = table_ref[which, 0], table_ref[which, 1]
    return dot(table_high, high) + (dot(table_low, high) + dot(table_high, low))


def put(high_ref, low_ref, index, at, left, right):
    high, low = split(jnp.concatenate([left, right], axis=1))
    high_ref[index, at : at + strip] = high
    low_ref[index, at : at + strip] = low


def beside(products, strips):
    count = len(products)
    for i, product in enumerate(products):
        product()
        for work in strips[i * len(strips) // count : (i + 1) * len(strips) // count]:
            work()


def step_stages(mode, core, refs):
    (probe_ref, window_ref, table_ref, a_high, a_low, b_high, b_low, mid_ref, near_ref, far_ref, sum_ref, obj_ref,
     mine_re_ref, mine_im_ref, peer_re_ref, peer_im_ref) = refs
    p = 2 * (mode % 2)

    def exits(r):
        at = slice(r, r + strip)
        probe_re, probe_im = probe_ref[0, mode, at].astype(f32), probe_ref[1, mode, at].astype(f32)
        win_re, win_im = window_ref[0, at], window_ref[1, at]
        re = probe_re * win_re - probe_im * win_im
        im = probe_re * win_im + probe_im * win_re
        put(a_high, a_low, p, r, re[:, :half] + re[:, half:], im[:, :half] + im[:, half:])
        put(a_high, a_low, p + 1, r, re[:, :half] - re[:, half:], im[:, :half] - im[:, half:])

    def far_columns(odd):
        mid_ref[p + odd] = data_by_table(a_high[p + odd], a_low[p + odd], table_ref, 4 + 2 * odd)

    def folds(r):
        even_top, even_bottom = mid_ref[p, r : r + strip], mid_ref[p, half + r : half + r + strip]
        odd_top, odd_bottom = mid_ref[p + 1, r : r + strip], mid_ref[p + 1, half + r : half + r + strip]
        for odd, even_fold, odd_fold in (
            (0, even_top + even_bottom, odd_top + odd_bottom),
            (1, even_top - even_bottom, odd_top - odd_bottom),
        ):
            put(b_high, b_low, p + odd, r, even_fold[:, :half], odd_fold[:, :half])
            put(b_high, b_low, p + odd, half + r, even_fold[:, half:], odd_fold[:, half:])

    def far_rows(odd):
        far_ref[mode, odd] = table_by_data(table_ref, 1 + 2 * odd, b_high[p + odd], b_low[p + odd])

    def sums(odd, r):
        re, im = far_ref[mode, odd, r : r + strip], far_ref[mode, odd, half + r : half + r + strip]
        sum_ref[odd, r : r + strip] += re * re + im * im

    def scale(odd, r):
        residual = sum_ref[odd, r : r + strip]
        for at in (r, half + r):
            scaled = far_ref[mode, odd, at : at + strip] * residual
            put(b_high, b_low, p + odd, at, scaled[:, :half], scaled[:, half:])

    def near_rows(odd):
        mid_ref[p + odd] = table_by_data(table_ref, 2 * odd, b_high[p + odd], b_low[p + odd])

    def unfolds(r):
        even_re, even_im = mid_ref[p, r : r + strip], mid_ref[p, half + r : half + r + strip]
        odd_re, odd_im = mid_ref[p + 1, r : r + strip], mid_ref[p + 1, half + r : half + r + strip]
        for at, re, im in ((r, even_re + odd_re, even_im + odd_im), (half + r, even_re - odd_re, even_im - odd_im)):
            put(a_high, a_low, p, at, re[:, :half], im[:, :half])
            put(a_high, a_low, p + 1, at, re[:, half:], im[:, half:])

    def near_columns(odd):
        near_ref[p + odd] = data_by_table(a_high[p + odd], a_low[p + odd], table_ref, 5 + 2 * odd)

    def grads(r):
        gradients(
            mode, r, core, probe_ref, window_ref, near_ref, obj_ref, mine_re_ref, mine_im_ref, peer_re_ref, peer_im_ref
        )

    both = range(2)
    long, short = range(0, full, strip), range(0, half, strip)
    ahead = (
        [functools.partial(exits, r) for r in long],
        [functools.partial(far_columns, odd) for odd in both],
        [functools.partial(folds, r) for r in short],
        [functools.partial(far_rows, odd) for odd in both],
        [functools.partial(sums, odd, r) for odd in both for r in short],
    )
    back = (
        [functools.partial(scale, odd, r) for odd in both for r in short],
        [functools.partial(near_rows, odd) for odd in both],
        [functools.partial(unfolds, r) for r in short],
        [functools.partial(near_columns, odd) for odd in both],
        [functools.partial(grads, r) for r in long],
    )
    return ahead, back


def pipelined(stages):
    none = ([], [], [], [], [])
    item = lambda i: stages[i] if 0 <= i < len(stages) else none
    for work in item(0)[0]:
        work()
    beside(item(0)[1], item(1)[0])
    for i in range(len(stages)):
        beside(item(i + 1)[1] or [lambda: None], item(i)[2])
        beside(item(i)[3], item(i - 1)[4] + item(i + 2)[0])
    for work in item(len(stages) - 1)[4]:
        work()


def reorder(x, order):
    high = x.astype(bf16)
    left = x - high.astype(f32)
    mid = left.astype(bf16)
    low = (left - mid.astype(f32)).astype(bf16)
    return dot(jnp.concatenate([high, mid, low], axis=1), jnp.concatenate([order, order, order], axis=0))


def store_strip(mine_ref, peer_ref, mode, r, left, right, core):
    z, x = r // strip // 4, r // strip % 4
    lanes = lax.broadcasted_iota(jnp.int32, (strip, half), 1)
    first = jnp.where(lanes < half // 2, left, pltpu.roll(right, half // 2, 1))
    second = jnp.where(lanes < half // 2, pltpu.roll(left, half // 2, 1), right)
    mine_ref[x, z, mode] = jnp.where(core == 0, first, second)
    peer_ref[x, z, mode] = jnp.where(core == 0, second, first)


def gradients(mode, r, core, probe_ref, window_ref, mid_ref, obj_ref, mine_re_ref, mine_im_ref, peer_re_ref, peer_im_ref):
    a = 2 * (mode % 2)
    at = slice(r, r + strip)
    even, odd = mid_ref[a, at], mid_ref[a + 1, at]
    up, down = even + odd, even - odd
    parts_re, parts_im = [], []
    for side, near in enumerate((up, down)):
        lanes = slice(side * half, side * half + half)
        near_re, near_im = near[:, :half], near[:, half:]
        probe_re, probe_im = probe_ref[0, mode, at, lanes].astype(f32), probe_ref[1, mode, at, lanes].astype(f32)
        win_re, win_im = window_ref[0, at, lanes], window_ref[1, at, lanes]
        parts_re.append(win_re * near_re + win_im * near_im)
        parts_im.append(win_re * near_im - win_im * near_re)
        obj_re = probe_re * near_re + probe_im * near_im
        obj_im = probe_re * near_im - probe_im * near_re
        if mode:
            obj_re = obj_re + obj_ref[0, at, lanes]
            obj_im = obj_im + obj_ref[1, at, lanes]
        obj_ref[0, at, lanes] = obj_re
        obj_ref[1, at, lanes] = obj_im
    store_strip(mine_re_ref, peer_re_ref, mode, r, *parts_re, core)
    store_strip(mine_im_ref, peer_im_ref, mode, r, *parts_im, core)


def cells():
    rows = lax.broadcasted_iota(jnp.int32, (full, full), 0)
    cols = lax.broadcasted_iota(jnp.int32, (full, full), 1)
    return rows, cols


def prepare_kernel(
    probe_in, intensity_in, table_in, order_in, probe_out, measured_out, table_out, order_out,
    probe_ref, intensity_ref, order_ref, sems,
):
    copies = [
        pltpu.make_async_copy(source, target, sems.at[i])
        for i, (source, target) in enumerate(
            [(order_in, order_ref), (intensity_in, intensity_ref), (probe_in, probe_ref), (table_in, table_out)]
        )
    ]
    for copy in copies:
        copy.start()
    copies[0].wait()
    copies[1].wait()
    frequencies, turned, shuffle = order_ref[0], order_ref[1], order_ref[2]
    measured_out[...] = dot(dot(frequencies, intensity_ref[...]).astype(bf16), turned)
    order_out[0] = shuffle
    order_out[1] = order_ref[3]
    copies[2].wait()
    for part in range(2):
        for mode in range(modes):
            probe_out[part, mode] = dot(probe_ref[part, mode], shuffle).astype(bf16)
    copies[3].wait()


def main_kernel(
    offset_ref, count_ref, own_ref, right_ref, lower_ref, probe_ref, measured_ref,
    table_ref, order_ref, mine_re_ref, mine_im_ref, peer_re_ref, peer_im_ref, stays_ref, moves_ref,
    window_ref, far_ref, a_high, a_low, b_high, b_low, mid_ref, near_ref, sum_ref, obj_ref,
):
    row_offset = offset_ref[0]
    col_offset = offset_ref[1]
    live = (count_ref[0] > 0).astype(f32)
    core = lax.axis_index("core")
    rows, cols = cells()
    in_row = rows >= row_offset
    in_col = cols >= col_offset
    for part in range(2):
        mixed = jnp.where(in_row, jnp.where(in_col, own_ref[part], right_ref[part]), lower_ref[part])
        mixed = pltpu.roll(mixed, lax.rem(full - row_offset, full), 0)
        window_ref[part] = reorder(pltpu.roll(mixed, lax.rem(full - col_offset, full), 1), order_ref[0])
    sum_ref[0] = -measured_ref[:half]
    sum_ref[1] = -measured_ref[half:]
    refs = (
        probe_ref, window_ref, table_ref, a_high, a_low, b_high, b_low, mid_ref, near_ref, far_ref, sum_ref, obj_ref,
        mine_re_ref, mine_im_ref, peer_re_ref, peer_im_ref,
    )
    stages = [step_stages(mode, core, refs) for mode in range(modes)]
    pipelined([ahead for ahead, back in stages])
    sum_ref[...] = sum_ref[...] * live
    pipelined([back for ahead, back in stages])
    for part in range(2):
        placed = reorder(obj_ref[part], order_ref[1])
        placed = pltpu.roll(pltpu.roll(placed, row_offset, 0), col_offset, 1)
        stays_ref[part] = jnp.where(in_col, placed, 0.0)
        moves_ref[part, :full] = jnp.where(in_col, 0.0, placed)
        moves_ref[part, full:] = jnp.zeros((8, full), f32) + row_offset.astype(f32)


def hold_kernel(tile_in, tile_out, sem):
    copy = pltpu.make_async_copy(tile_in, tile_out, sem)
    copy.start()
    copy.wait()


def mix_kernel(offset_ref, own_ref, right_ref, out_ref):
    rows, cols = cells()
    in_col = cols >= offset_ref[1]
    for part in range(2):
        out_ref[part] = jnp.where(in_col, own_ref[part], right_ref[part])


def down_kernel(offset_ref, stays_ref, moved_ref, down_ref, held_ref):
    rows, cols = cells()
    in_row = rows >= offset_ref[0]
    left_in_row = rows.astype(f32) >= moved_ref[0, full : full + 1]
    for part in range(2):
        stays, moved = stays_ref[part], moved_ref[part, :full]
        down_ref[part] = jnp.where(in_row, 0.0, stays) + jnp.where(left_in_row, 0.0, moved)
        held_ref[part] = jnp.where(in_row, stays, 0.0) + jnp.where(left_in_row, moved, 0.0)


def cores_kernel(mine_ref, theirs_ref, send_ref, keep_ref):
    x = lax.axis_index("x")
    core = lax.axis_index("core")
    first = jnp.where(core == 0, x ^ 1, 3 - x)
    second = jnp.where(core == 0, 3 - x, x ^ 1)
    for ref, slot, index in ((send_ref, 0, first), (send_ref, 1, x ^ 2), (keep_ref, 0, x), (keep_ref, 1, second)):
        ref[slot] = mine_ref[index] + theirs_ref[index]


def columns_kernel(kept_re, got_re, came_re, kept_im, got_im, came_im, out_ref):
    for part, (kept_ref, got_ref, came_ref) in enumerate(((kept_re, got_re, came_re), (kept_im, got_im, came_im))):
        for z in range(4):
            turned = (kept_ref[0, z] + got_ref[0, z] + came_ref[z]).reshape(96, half).T
            lane = z * 192 + part * 96
            for y in range(8):
                for z_hi in range(2):
                    at = z_hi * 64 + y * 8
                    out_ref[y, z_hi * 8 : z_hi * 8 + 8, lane : lane + 96] = turned[at : at + 8]


def depth_kernel(parts_ref, out_ref):
    total = parts_ref[0]
    for i in range(1, 8):
        total = total + parts_ref[i]
    for z in range(4):
        for z_hi in range(2):
            out_ref[2 * z + z_hi] = total[z_hi * 8 : z_hi * 8 + 8, z * 192 : z * 192 + 192]


def finish_kernel(parts_ref, own_ref, out_ref):
    total = parts_ref[0]
    for i in range(1, 8):
        total = total + parts_ref[i]
    for part in range(2):
        for mode in range(modes):
            at = (part * modes + mode) * strip
            out_ref[part, mode] = own_ref[part, mode] - (512.0 ** -0.5) * total[:, at : at + strip]


def shaped(*shape, dtype=f32):
    return jax.ShapeDtypeStruct(shape, dtype)


step_scratch = [pltpu.VMEM((4, full, full), bf16)] * 4 + [
    pltpu.VMEM((4, full, full), f32),
    pltpu.VMEM((4, full, full), f32),
    pltpu.VMEM((2, half, full), f32),
    pltpu.VMEM((2, full, full), f32),
]
vmem = pl.BlockSpec(memory_space=pltpu.VMEM)
smem = pl.BlockSpec(memory_space=pltpu.SMEM)


def call(kernel, name, inputs, outputs, scratch=(), flops=0, moved=0, limit=4):
    return pl.pallas_call(
        kernel,
        out_shape=tuple(outputs) if len(outputs) > 1 else outputs[0],
        in_specs=inputs,
        out_specs=(vmem,) * len(outputs) if len(outputs) > 1 else vmem,
        scratch_shapes=scratch,
        compiler_params=pltpu.CompilerParams(vmem_limit_bytes=limit * 1024 * 1024),
        cost_estimate=pl.CostEstimate(flops=flops, bytes_accessed=moved, transcendentals=0),
        name=name,
    )


def local(object_field, probe_modes, offsets, counts, intensity):
    rows = ("z_lo", "x")
    cols = ("z_hi", "y", "core")
    tables, orders = halves_tables()
    right = passed_along(object_field, cols, -1)
    above_offset = passed_along(offsets, rows, 1).reshape(2)
    above_offset, tile = lax.optimization_barrier((above_offset, object_field))
    own = call(
        hold_kernel, "hold", [pl.BlockSpec(memory_space=pl.ANY)], [shaped(2, full, full)],
        scratch=[pltpu.SemaphoreType.DMA], moved=1_000_000,
    )(tile)
    mixed = call(mix_kernel, "mix", [smem, vmem, vmem], [shaped(2, full, full)], moved=2_000_000)(
        above_offset, own, right
    )
    lower = passed_along(mixed, rows, -1)
    start = (0, 0, lax.axis_index(rows) * strip, lax.axis_index(cols) * 8)
    own_probe = lax.dynamic_slice(probe_modes, start, (2, modes, strip, 8)).astype(f32)
    probe, measured, table, order = call(
        prepare_kernel,
        "prepare",
        [pl.BlockSpec(memory_space=pl.ANY)] * 4,
        [
            shaped(2, modes, full, full, dtype=bf16),
            shaped(full, full),
            shaped(8, 2, full, full, dtype=bf16),
            shaped(2, full, full, dtype=bf16),
        ],
        scratch=[
            pltpu.VMEM((2, modes, full, full), bf16),
            pltpu.VMEM((full, full), bf16),
            pltpu.VMEM((4, full, full), bf16),
            pltpu.SemaphoreType.DMA((4,)),
        ],
        flops=500_000_000,
        moved=8_000_000,
        limit=6,
    )(probe_modes, intensity[0, 0, 0], jnp.asarray(tables), jnp.asarray(orders))
    block_shape = (4, 4, modes, strip, half)
    mine_re, mine_im, peer_re, peer_im, stays, moves = call(
        main_kernel,
        "step",
        [smem, smem] + [vmem] * 7,
        [shaped(*block_shape)] * 4 + [shaped(2, full, full), shaped(2, full + 8, full)],
        scratch=[pltpu.VMEM((2, full, full), f32), pltpu.VMEM((modes, 2, full, full), f32), *step_scratch],
        flops=5_000_000_000,
        moved=12_000_000,
        limit=14,
    )(offsets.reshape(2), counts.reshape(1), own, right, lower, probe, measured, table, order)

    near_pairs = [(2 * x + c, 2 * ((x ^ 1) if c == 0 else 3 - x) + c) for x in range(4) for c in range(2)]
    far_pairs = [(2 * x + c, 2 * (3 - x if c == 0 else (x ^ 1)) + c) for x in range(4) for c in range(2)]
    half_shape = (2, *block_shape[1:])
    summed = []
    theirs = [lax.ppermute(peer, "core", [(0, 1), (1, 0)]) for peer in (peer_re, peer_im)]
    for mine, other in zip((mine_re, mine_im), theirs):
        send, keep = call(
            cores_kernel, "add_cores", [vmem] * 2, [shaped(*half_shape)] * 2, moved=3_000_000
        )(mine, other)
        summed.append((keep, lax.ppermute(send, ("x", "core"), near_pairs)))
    from_left = passed_along(moves, cols, 1)
    arrived = []
    for keep, got in summed:
        arrived += [keep, got, lax.ppermute(keep[1] + got[1], ("x", "core"), far_pairs)]
    packed = call(columns_kernel, "add_columns", [vmem] * 6, [shaped(8, strip, 768)], moved=2_000_000)(*arrived)
    stays, _ = lax.optimization_barrier((stays, packed))
    down, held = call(down_kernel, "down", [smem, vmem, vmem], [shaped(2, full, full)] * 2, moved=2_000_000)(
        offsets.reshape(2), stays, from_left
    )
    from_above = passed_along(down, rows, 1)
    parts = lax.all_to_all(packed, "y", 0, 0, tiled=True)
    packed = call(depth_kernel, "add_depth", [vmem], [shaped(8, 8, 192)], moved=500_000)(parts)
    parts = lax.all_to_all(packed, ("z_lo", "z_hi"), 0, 0, tiled=True)
    probe_new = call(finish_kernel, "finish", [vmem] * 2, [shaped(2, modes, 8, strip)], moved=200_000)(
        parts, own_probe.transpose(0, 1, 3, 2)
    ).transpose(0, 1, 3, 2)

    object_new = object_field - object_rate * (held + from_above)
    return (object_new, probe_new)


def solution(mesh):
    grid = jax.sharding.Mesh(mesh.devices.reshape(4, 4, 2, 8, 2), ("z_lo", "x", "z_hi", "y", "core"))
    rows = ("z_lo", "x")
    cols = ("z_hi", "y", "core")
    in_specs = (
        P(None, rows, cols),
        P(),
        P(rows, cols, None, None),
        P(rows, cols),
        P(rows, cols, None, None, None),
    )
    out_specs = (P(None, rows, cols), P(None, None, rows, cols))
    return jax.shard_map(local, mesh=grid, in_specs=in_specs, out_specs=out_specs, check_vma=False)
```

```python
import functools
import math

import jax
import jax.numpy as jnp
import ml_dtypes
import numpy as np
from jax import lax
from jax.experimental import pallas as pl
from jax.experimental.pallas import tpu as pltpu
from jax.sharding import PartitionSpec as P

object_rate = 0.25
f32 = jnp.float32
bf16 = jnp.bfloat16
half = 128
full = 256
modes = 6
strip = 16


def passed_along(x, axis, by):
    devices = lax.axis_size(axis)
    pairs = [(i, i + by) for i in range(devices) if 0 <= i + by < devices]
    return lax.ppermute(x, axis, pairs)


def halves_tables():
    place = np.arange(half)[:, None]
    freq = np.arange(half)[None, :]
    columns = column_order()[:half]
    tables = []
    for places in (place, columns[:, None]):
        for odd in (0, 1):
            angle = -2.0 * math.pi * ((places * (2 * freq + odd)) % full) / full
            re, im = np.cos(angle) / 16.0, np.sin(angle) / 16.0
            real_form = np.block([[re, im], [-im, re]]).astype(np.float32)
            for form in (real_form, real_form.T):
                high = form.astype(ml_dtypes.bfloat16)
                low = (form - high.astype(np.float32)).astype(ml_dtypes.bfloat16)
                tables.append(np.stack([high, low]))
    frequencies = np.zeros((full, full), np.float32)
    shuffle = np.zeros((full, full), np.float32)
    for k in range(full):
        frequencies[(k % 2) * half + k // 2, k] = 1.0
    shuffle[column_order(), np.arange(full)] = 1.0
    orders = np.stack([frequencies, frequencies.T, shuffle, shuffle.T])
    return np.stack(tables), orders.astype(ml_dtypes.bfloat16)


def column_order():
    columns = np.arange(full).reshape(2, 8, 2, 8)
    return columns.transpose(0, 2, 1, 3).reshape(-1)


def split(x):
    high = x.astype(bf16)
    return high, (x - high.astype(f32)).astype(bf16)


def dot(a, b):
    return jnp.dot(a, b, preferred_element_type=f32)


def data_by_table(high, low, table_ref, which):
    table_high, table_low = table_ref[which, 0], table_ref[which, 1]
    return dot(high, table_high) + (dot(high, table_low) + dot(low, table_high))


def table_by_data(table_ref, which, high, low):
    table_high, table_low = table_ref[which, 0], table_ref[which, 1]
    return dot(table_high, high) + (dot(table_low, high) + dot(table_high, low))


def put(high_ref, low_ref, index, at, left, right):
    high, low = split(jnp.concatenate([left, right], axis=1))
    high_ref[index, at : at + strip] = high
    low_ref[index, at : at + strip] = low


def beside(products, strips):
    count = len(products)
    for i, product in enumerate(products):
        product()
        for work in strips[i * len(strips) // count : (i + 1) * len(strips) // count]:
            work()


def step_stages(mode, core, refs):
    (probe_ref, window_ref, table_ref, a_high, a_low, b_high, b_low, mid_ref, near_ref, far_ref, sum_ref, obj_ref,
     mine_re_ref, mine_im_ref, peer_re_ref, peer_im_ref) = refs
    p = 2 * (mode % 2)

    def exits(r):
        at = slice(r, r + strip)
        probe_re, probe_im = probe_ref[0, mode, at].astype(f32), probe_ref[1, mode, at].astype(f32)
        win_re, win_im = window_ref[0, at], window_ref[1, at]
        re = probe_re * win_re - probe_im * win_im
        im = probe_re * win_im + probe_im * win_re
        put(a_high, a_low, p, r, re[:, :half] + re[:, half:], im[:, :half] + im[:, half:])
        put(a_high, a_low, p + 1, r, re[:, :half] - re[:, half:], im[:, :half] - im[:, half:])

    def far_columns(odd):
        mid_ref[p + odd] = data_by_table(a_high[p + odd], a_low[p + odd], table_ref, 4 + 2 * odd)

    def folds(r):
        even_top, even_bottom = mid_ref[p, r : r + strip], mid_ref[p, half + r : half + r + strip]
        odd_top, odd_bottom = mid_ref[p + 1, r : r + strip], mid_ref[p + 1, half + r : half + r + strip]
        for odd, even_fold, odd_fold in (
            (0, even_top + even_bottom, odd_top + odd_bottom),
            (1, even_top - even_bottom, odd_top - odd_bottom),
        ):
            put(b_high, b_low, p + odd, r, even_fold[:, :half], odd_fold[:, :half])
            put(b_high, b_low, p + odd, half + r, even_fold[:, half:], odd_fold[:, half:])

    def far_rows(odd):
        far_ref[mode, odd] = table_by_data(table_ref, 1 + 2 * odd, b_high[p + odd], b_low[p + odd])

    def sums(odd, r):
        re, im = far_ref[mode, odd, r : r + strip], far_ref[mode, odd, half + r : half + r + strip]
        sum_ref[odd, r : r + strip] += re * re + im * im

    def scale(odd, r):
        residual = sum_ref[odd, r : r + strip]
        for at in (r, half + r):
            scaled = far_ref[mode, odd, at : at + strip] * residual
            put(b_high, b_low, p + odd, at, scaled[:, :half], scaled[:, half:])

    def near_rows(odd):
        mid_ref[p + odd] = table_by_data(table_ref, 2 * odd, b_high[p + odd], b_low[p + odd])

    def unfolds(r):
        even_re, even_im = mid_ref[p, r : r + strip], mid_ref[p, half + r : half + r + strip]
        odd_re, odd_im = mid_ref[p + 1, r : r + strip], mid_ref[p + 1, half + r : half + r + strip]
        for at, re, im in ((r, even_re + odd_re, even_im + odd_im), (half + r, even_re - odd_re, even_im - odd_im)):
            put(a_high, a_low, p, at, re[:, :half], im[:, :half])
            put(a_high, a_low, p + 1, at, re[:, half:], im[:, half:])

    def near_columns(odd):
        near_ref[p + odd] = data_by_table(a_high[p + odd], a_low[p + odd], table_ref, 5 + 2 * odd)

    def grads(r):
        gradients(
            mode, r, core, probe_ref, window_ref, near_ref, obj_ref, mine_re_ref, mine_im_ref, peer_re_ref, peer_im_ref
        )

    both = range(2)
    long, short = range(0, full, strip), range(0, half, strip)
    ahead = (
        [functools.partial(exits, r) for r in long],
        [functools.partial(far_columns, odd) for odd in both],
        [functools.partial(folds, r) for r in short],
        [functools.partial(far_rows, odd) for odd in both],
        [functools.partial(sums, odd, r) for odd in both for r in short],
    )
    back = (
        [functools.partial(scale, odd, r) for odd in both for r in short],
        [functools.partial(near_rows, odd) for odd in both],
        [functools.partial(unfolds, r) for r in short],
        [functools.partial(near_columns, odd) for odd in both],
        [functools.partial(grads, r) for r in long],
    )
    return ahead, back


def pipelined(stages):
    none = ([], [], [], [], [])
    item = lambda i: stages[i] if 0 <= i < len(stages) else none
    for work in item(0)[0]:
        work()
    beside(item(0)[1], item(1)[0])
    for i in range(len(stages)):
        beside(item(i + 1)[1] or [lambda: None], item(i)[2])
        beside(item(i)[3], item(i - 1)[4] + item(i + 2)[0])
    for work in item(len(stages) - 1)[4]:
        work()


def reorder(x, order):
    high = x.astype(bf16)
    left = x - high.astype(f32)
    mid = left.astype(bf16)
    low = (left - mid.astype(f32)).astype(bf16)
    return dot(jnp.concatenate([high, mid, low], axis=1), jnp.concatenate([order, order, order], axis=0))


def store_strip(mine_ref, peer_ref, mode, r, left, right, core):
    z, x = r // strip // 4, r // strip % 4
    lanes = lax.broadcasted_iota(jnp.int32, (strip, half), 1)
    first = jnp.where(lanes < half // 2, left, pltpu.roll(right, half // 2, 1))
    second = jnp.where(lanes < half // 2, pltpu.roll(left, half // 2, 1), right)
    mine_ref[x, z, mode] = jnp.where(core == 0, first, second)
    peer_ref[x, z, mode] = jnp.where(core == 0, second, first)


def gradients(mode, r, core, probe_ref, window_ref, mid_ref, obj_ref, mine_re_ref, mine_im_ref, peer_re_ref, peer_im_ref):
    a = 2 * (mode % 2)
    at = slice(r, r + strip)
    even, odd = mid_ref[a, at], mid_ref[a + 1, at]
    up, down = even + odd, even - odd
    parts_re, parts_im = [], []
    for side, near in enumerate((up, down)):
        lanes = slice(side * half, side * half + half)
        near_re, near_im = near[:, :half], near[:, half:]
        probe_re, probe_im = probe_ref[0, mode, at, lanes].astype(f32), probe_ref[1, mode, at, lanes].astype(f32)
        win_re, win_im = window_ref[0, at, lanes], window_ref[1, at, lanes]
        parts_re.append(win_re * near_re + win_im * near_im)
        parts_im.append(win_re * near_im - win_im * near_re)
        obj_re = probe_re * near_re + probe_im * near_im
        obj_im = probe_re * near_im - probe_im * near_re
        if mode:
            obj_re = obj_re + obj_ref[0, at, lanes]
            obj_im = obj_im + obj_ref[1, at, lanes]
        obj_ref[0, at, lanes] = obj_re
        obj_ref[1, at, lanes] = obj_im
    store_strip(mine_re_ref, peer_re_ref, mode, r, *parts_re, core)
    store_strip(mine_im_ref, peer_im_ref, mode, r, *parts_im, core)


def cells():
    rows = lax.broadcasted_iota(jnp.int32, (full, full), 0)
    cols = lax.broadcasted_iota(jnp.int32, (full, full), 1)
    return rows, cols


def prepare_kernel(
    probe_in, intensity_in, table_in, order_in, probe_out, measured_out, table_out, order_out,
    probe_ref, intensity_ref, order_ref, sems,
):
    copies = [
        pltpu.make_async_copy(source, target, sems.at[i])
        for i, (source, target) in enumerate(
            [(order_in, order_ref), (intensity_in, intensity_ref), (probe_in, probe_ref), (table_in, table_out)]
        )
    ]
    for copy in copies:
        copy.start()
    copies[0].wait()
    copies[1].wait()
    frequencies, turned, shuffle = order_ref[0], order_ref[1], order_ref[2]
    measured_out[...] = dot(dot(frequencies, intensity_ref[...]).astype(bf16), turned)
    order_out[0] = shuffle
    order_out[1] = order_ref[3]
    copies[2].wait()
    for part in range(2):
        for mode in range(modes):
            probe_out[part, mode] = dot(probe_ref[part, mode], shuffle).astype(bf16)
    copies[3].wait()


def main_kernel(
    offset_ref, count_ref, own_ref, right_ref, lower_ref, probe_ref, measured_ref,
    table_ref, order_ref, mine_re_ref, mine_im_ref, peer_re_ref, peer_im_ref, stays_ref, moves_ref,
    window_ref, far_ref, a_high, a_low, b_high, b_low, mid_ref, near_ref, sum_ref, obj_ref,
):
    row_offset = offset_ref[0]
    col_offset = offset_ref[1]
    live = (count_ref[0] > 0).astype(f32)
    core = lax.axis_index("core")
    rows, cols = cells()
    in_row = rows >= row_offset
    in_col = cols >= col_offset
    for part in range(2):
        mixed = jnp.where(in_row, jnp.where(in_col, own_ref[part], right_ref[part]), lower_ref[part])
        mixed = pltpu.roll(mixed, lax.rem(full - row_offset, full), 0)
        window_ref[part] = reorder(pltpu.roll(mixed, lax.rem(full - col_offset, full), 1), order_ref[0])
    sum_ref[0] = -measured_ref[:half]
    sum_ref[1] = -measured_ref[half:]
    refs = (
        probe_ref, window_ref, table_ref, a_high, a_low, b_high, b_low, mid_ref, near_ref, far_ref, sum_ref, obj_ref,
        mine_re_ref, mine_im_ref, peer_re_ref, peer_im_ref,
    )
    stages = [step_stages(mode, core, refs) for mode in range(modes)]
    pipelined([ahead for ahead, back in stages])
    sum_ref[...] = sum_ref[...] * live
    pipelined([back for ahead, back in stages])
    for part in range(2):
        placed = reorder(obj_ref[part], order_ref[1])
        placed = pltpu.roll(pltpu.roll(placed, row_offset, 0), col_offset, 1)
        stays_ref[part] = jnp.where(in_col, placed, 0.0)
        moves_ref[part, :full] = jnp.where(in_col, 0.0, placed)
        moves_ref[part, full:] = jnp.zeros((8, full), f32) + row_offset.astype(f32)


def hold_kernel(tile_in, tile_out, sem):
    copy = pltpu.make_async_copy(tile_in, tile_out, sem)
    copy.start()
    copy.wait()


def mix_kernel(offset_ref, own_ref, right_ref, out_ref):
    rows, cols = cells()
    in_col = cols >= offset_ref[1]
    for part in range(2):
        out_ref[part] = jnp.where(in_col, own_ref[part], right_ref[part])


def down_kernel(offset_ref, stays_ref, moved_ref, down_ref, held_ref):
    rows, cols = cells()
    in_row = rows >= offset_ref[0]
    left_in_row = rows.astype(f32) >= moved_ref[0, full : full + 1]
    for part in range(2):
        stays, moved = stays_ref[part], moved_ref[part, :full]
        down_ref[part] = jnp.where(in_row, 0.0, stays) + jnp.where(left_in_row, 0.0, moved)
        held_ref[part] = jnp.where(in_row, stays, 0.0) + jnp.where(left_in_row, moved, 0.0)


def cores_kernel(mine_ref, theirs_ref, send_ref, keep_ref):
    x = lax.axis_index("x")
    core = lax.axis_index("core")
    first = jnp.where(core == 0, x ^ 1, 3 - x)
    second = jnp.where(core == 0, 3 - x, x ^ 1)
    for ref, slot, index in ((send_ref, 0, first), (send_ref, 1, x ^ 2), (keep_ref, 0, x), (keep_ref, 1, second)):
        ref[slot] = mine_ref[index] + theirs_ref[index]


def columns_kernel(kept_re, got_re, came_re, kept_im, got_im, came_im, out_ref):
    pieces = []
    for z in range(4):
        for kept_ref, got_ref, came_ref in ((kept_re, got_re, came_re), (kept_im, got_im, came_im)):
            pieces.append((kept_ref[0, z] + got_ref[0, z] + came_ref[z]).reshape(96, half))
    turned = jnp.concatenate(pieces, axis=0).T
    for y in range(8):
        for z_hi in range(2):
            at = z_hi * 64 + y * 8
            out_ref[y, z_hi * 8 : z_hi * 8 + 8] = turned[at : at + 8]


def depth_kernel(parts_ref, out_ref):
    total = parts_ref[0]
    for i in range(1, 8):
        total = total + parts_ref[i]
    for z in range(4):
        for z_hi in range(2):
            out_ref[2 * z + z_hi] = total[z_hi * 8 : z_hi * 8 + 8, z * 192 : z * 192 + 192]


def finish_kernel(parts_ref, own_ref, out_ref):
    total = parts_ref[0]
    for i in range(1, 8):
        total = total + parts_ref[i]
    for part in range(2):
        for mode in range(modes):
            at = (part * modes + mode) * strip
            out_ref[part, mode] = own_ref[part, mode] - (512.0 ** -0.5) * total[:, at : at + strip]


def shaped(*shape, dtype=f32):
    return jax.ShapeDtypeStruct(shape, dtype)


step_scratch = [pltpu.VMEM((4, full, full), bf16)] * 4 + [
    pltpu.VMEM((4, full, full), f32),
    pltpu.VMEM((4, full, full), f32),
    pltpu.VMEM((2, half, full), f32),
    pltpu.VMEM((2, full, full), f32),
]
vmem = pl.BlockSpec(memory_space=pltpu.VMEM)
smem = pl.BlockSpec(memory_space=pltpu.SMEM)


def call(kernel, name, inputs, outputs, scratch=(), flops=0, moved=0, limit=4):
    return pl.pallas_call(
        kernel,
        out_shape=tuple(outputs) if len(outputs) > 1 else outputs[0],
        in_specs=inputs,
        out_specs=(vmem,) * len(outputs) if len(outputs) > 1 else vmem,
        scratch_shapes=scratch,
        compiler_params=pltpu.CompilerParams(vmem_limit_bytes=limit * 1024 * 1024),
        cost_estimate=pl.CostEstimate(flops=flops, bytes_accessed=moved, transcendentals=0),
        name=name,
    )


def local(object_field, probe_modes, offsets, counts, intensity):
    rows = ("z_lo", "x")
    cols = ("z_hi", "y", "core")
    tables, orders = halves_tables()
    right = passed_along(object_field, cols, -1)
    above_offset = passed_along(offsets, rows, 1).reshape(2)
    above_offset, tile = lax.optimization_barrier((above_offset, object_field))
    own = call(
        hold_kernel, "hold", [pl.BlockSpec(memory_space=pl.ANY)], [shaped(2, full, full)],
        scratch=[pltpu.SemaphoreType.DMA], moved=1_000_000,
    )(tile)
    mixed = call(mix_kernel, "mix", [smem, vmem, vmem], [shaped(2, full, full)], moved=2_000_000)(
        above_offset, own, right
    )
    lower = passed_along(mixed, rows, -1)
    start = (0, 0, lax.axis_index(rows) * strip, lax.axis_index(cols) * 8)
    own_probe = lax.dynamic_slice(probe_modes, start, (2, modes, strip, 8)).astype(f32)
    probe, measured, table, order = call(
        prepare_kernel,
        "prepare",
        [pl.BlockSpec(memory_space=pl.ANY)] * 4,
        [
            shaped(2, modes, full, full, dtype=bf16),
            shaped(full, full),
            shaped(8, 2, full, full, dtype=bf16),
            shaped(2, full, full, dtype=bf16),
        ],
        scratch=[
            pltpu.VMEM((2, modes, full, full), bf16),
            pltpu.VMEM((full, full), bf16),
            pltpu.VMEM((4, full, full), bf16),
            pltpu.SemaphoreType.DMA((4,)),
        ],
        flops=500_000_000,
        moved=8_000_000,
        limit=6,
    )(probe_modes, intensity[0, 0, 0], jnp.asarray(tables), jnp.asarray(orders))
    block_shape = (4, 4, modes, strip, half)
    mine_re, mine_im, peer_re, peer_im, stays, moves = call(
        main_kernel,
        "step",
        [smem, smem] + [vmem] * 7,
        [shaped(*block_shape)] * 4 + [shaped(2, full, full), shaped(2, full + 8, full)],
        scratch=[pltpu.VMEM((2, full, full), f32), pltpu.VMEM((modes, 2, full, full), f32), *step_scratch],
        flops=5_000_000_000,
        moved=12_000_000,
        limit=14,
    )(offsets.reshape(2), counts.reshape(1), own, right, lower, probe, measured, table, order)

    near_pairs = [(2 * x + c, 2 * ((x ^ 1) if c == 0 else 3 - x) + c) for x in range(4) for c in range(2)]
    far_pairs = [(2 * x + c, 2 * (3 - x if c == 0 else (x ^ 1)) + c) for x in range(4) for c in range(2)]
    half_shape = (2, *block_shape[1:])
    summed = []
    theirs = [lax.ppermute(peer, "core", [(0, 1), (1, 0)]) for peer in (peer_re, peer_im)]
    for mine, other in zip((mine_re, mine_im), theirs):
        send, keep = call(
            cores_kernel, "add_cores", [vmem] * 2, [shaped(*half_shape)] * 2, moved=3_000_000
        )(mine, other)
        summed.append((keep, lax.ppermute(send, ("x", "core"), near_pairs)))
    from_left = passed_along(moves, cols, 1)
    arrived = []
    for keep, got in summed:
        arrived += [keep, got, lax.ppermute(keep[1] + got[1], ("x", "core"), far_pairs)]
    packed = call(columns_kernel, "add_columns", [vmem] * 6, [shaped(8, strip, 768)], moved=2_000_000)(*arrived)
    stays, _ = lax.optimization_barrier((stays, packed))
    down, held = call(down_kernel, "down", [smem, vmem, vmem], [shaped(2, full, full)] * 2, moved=2_000_000)(
        offsets.reshape(2), stays, from_left
    )
    from_above = passed_along(down, rows, 1)
    parts = lax.all_to_all(packed, "y", 0, 0, tiled=True)
    packed = call(depth_kernel, "add_depth", [vmem], [shaped(8, 8, 192)], moved=500_000)(parts)
    parts = lax.all_to_all(packed, ("z_lo", "z_hi"), 0, 0, tiled=True)
    probe_new = call(finish_kernel, "finish", [vmem] * 2, [shaped(2, modes, 8, strip)], moved=200_000)(
        parts, own_probe.transpose(0, 1, 3, 2)
    ).transpose(0, 1, 3, 2)

    object_new = object_field - object_rate * (held + from_above)
    return (object_new, probe_new)


def solution(mesh):
    grid = jax.sharding.Mesh(mesh.devices.reshape(4, 4, 2, 8, 2), ("z_lo", "x", "z_hi", "y", "core"))
    rows = ("z_lo", "x")
    cols = ("z_hi", "y", "core")
    in_specs = (
        P(None, rows, cols),
        P(),
        P(rows, cols, None, None),
        P(rows, cols),
        P(rows, cols, None, None, None),
    )
    out_specs = (P(None, rows, cols), P(None, None, rows, cols))
    return jax.shard_map(local, mesh=grid, in_specs=in_specs, out_specs=out_specs, check_vma=False)
```
